256 devices in a mesh: tm: 8 (over x, core), space: 32 (over y, z).
Axes of the slice: x: 4, y: 4, z: 8, core: 2. Of those that a mesh axis runs over, the one named last changes fastest.
Arguments:
- queries: bfloat16 [32768, 4096], P(('tm', 'space')), may hold values from -4.5 to 4.5
- key_rows: bfloat16 [32768, 4096], P(('tm', 'space')), may hold values from -4.5 to 4.5
- value_rows: bfloat16 [32768, 4096], P(('tm', 'space')), may hold values from -6 to 6
- grads_out: bfloat16 [32768, 4096], P(('tm', 'space')), may hold values from -12 to 12
- block_lists: int32 [8, 32, 13], P('tm'), may hold values from 0 to 255, as said below
- block_counts: int32 [8, 32], P('tm'), may hold values from 1 to 13
Outputs:
- grad_queries: bfloat16 [32768, 4096], P(('tm', 'space'))
- grad_keys: bfloat16 [32768, 4096], P(('tm', 'space'))
- grad_values: bfloat16 [32768, 4096], P(('tm', 'space'))
The draws below stay inside these ranges and needn't reach their ends.
Inputs may be any that keep to these rules, and one draw needn't show every extreme that they name: For c < block_counts[f, i], block_lists[f, i, c] names distinct blocks g * 32 + j with |g - f| <= 2 and |j - i| <= 2 - |g - f|; every list names the block f * 32 + i; slots from block_counts[f, i] on hold f * 32 + i.
All inputs are finite; a program needn't handle non-finite values.
Results may differ from the reference program's by a relative error of at most 0.022.
Values may be sent and summed in bfloat16 or wider, within the bound.
A program may use at most 192 MiB of HBM per device.

```python
import jax
import jax.numpy as jnp
import numpy as np
from jax import lax

HEADS = 32
HD = 128
BLK = 128
LIST = 13
D = 4096
FRAMES = 8
FRAME = 4096
NQB = 32
TOKENS = 32768


def band_tables(key):
    key = jax.random.fold_in(key, 202)
    width_key, frame_key, block_key, order_key = jax.random.split(key, 4)
    shifts = [(step_frame, step_block) for step_frame in (-2, -1, 0, 1, 2) for step_block in range(abs(step_frame) - 2, 3 - abs(step_frame))]
    frame_step = jnp.array(np.array([entry[0] for entry in shifts], np.int32))
    block_step = jnp.array(np.array([entry[1] for entry in shifts], np.int32))
    caps = jnp.array(np.array([0, 1, 2, 1, 0], np.int32))
    widths = jax.random.randint(width_key, (FRAMES, NQB, 5), 0, caps + 1)
    chosen_frame = jax.random.randint(frame_key, (), 2, max(3, FRAMES - 2))
    chosen_block = jax.random.randint(block_key, (), 2, NQB - 2)
    frame_grid = jnp.arange(FRAMES, dtype=jnp.int32)[:, None, None]
    block_grid = jnp.arange(NQB, dtype=jnp.int32)[None, :, None]
    forced = (frame_grid == chosen_frame) & (block_grid == chosen_block)
    widths = jnp.where(forced, caps, widths)
    reach = widths[:, :, frame_step + 2]
    target_frame = frame_grid + frame_step
    target_block = block_grid + block_step
    valid = (jnp.abs(block_step) <= reach) & (target_frame >= 0) & (target_frame < FRAMES) & (target_block >= 0) & (target_block < NQB)
    own_block = frame_grid * NQB + block_grid
    entries = jnp.where(valid, target_frame * NQB + target_block, own_block)
    noise = jax.random.randint(order_key, (FRAMES, NQB, LIST), 0, 64)
    ranking = jnp.where(valid, 0, 100000) + noise * LIST + jnp.arange(LIST, dtype=jnp.int32)
    order = jnp.argsort(ranking, axis=-1)
    ordered = jnp.take_along_axis(entries, order, axis=-1)
    return (ordered.astype(jnp.int32), jnp.sum(valid.astype(jnp.int32), axis=-1).astype(jnp.int32))


def draw_queries(key, part):
    key = jax.random.fold_in(key, 1)
    return jnp.clip(jax.random.normal(key, (TOKENS, HEADS * HD), jnp.float32), -4.0, 4.0).astype(jnp.bfloat16)


def draw_key_rows(key, part):
    key = jax.random.fold_in(key, 2)
    return jnp.clip(jax.random.normal(key, (TOKENS, HEADS * HD), jnp.float32), -4.0, 4.0).astype(jnp.bfloat16)


def draw_block_lists(key, part):
    return band_tables(key)[0]


def draw_block_counts(key, part):
    return band_tables(key)[1]


def block_scale(rng, extent, shards, smallest, largest):
    factor_of = 1.0
    for axis_at, shards_of in shards:
        heights = jax.random.uniform(jax.random.fold_in(jax.random.fold_in(rng, 6), axis_at), (shards_of,), jnp.float32, smallest / len(shards), largest / len(shards))
        factor_of = factor_of * jnp.repeat(jnp.exp(heights), extent[axis_at] // shards_of).reshape((-1,) + (1,) * (len(extent) - 1 - axis_at))
    return factor_of


def centred(own_key, shape, spread, limit, pieces=(), kind=jnp.bfloat16):
    drawn = jax.random.normal(own_key, shape, jnp.float32) * spread
    if len(pieces) > 0:
        drawn = block_scale(own_key, shape, pieces, -0.22, 0.18) * drawn
    return jnp.clip(drawn, min=-limit, max=limit).astype(kind)


def setup_inputs(seed: int = 0) -> dict:
    keys = jax.random.split(jax.random.key(seed), 7)
    queries = draw_queries(jax.random.fold_in(keys[6], 71), 0)
    key_rows = draw_key_rows(jax.random.fold_in(keys[6], 71), 0)
    value_rows = centred(keys[2], (TOKENS, D), 1.0, 6.0, ((0, 256),))
    grads_out = centred(keys[3], (TOKENS, D), 2.0, 12.0, ((0, 256),))
    block_lists = draw_block_lists(jax.random.fold_in(keys[6], 71), 0)
    block_counts = draw_block_counts(jax.random.fold_in(keys[6], 71), 0)
    return {"queries": queries, "key_rows": key_rows, "value_rows": value_rows, "grads_out": grads_out, "block_lists": block_lists, "block_counts": block_counts}


def exact_product(pattern, first_op, second_op):
    return jnp.einsum(pattern, first_op.astype(jnp.float32), second_op.astype(jnp.float32))


def band_grads(queries, grads_out, key_rows, value_rows, block_ids, counts, block_len, head_dim, product):
    frame_len, width = queries.shape
    head_count = width // head_dim
    query_blocks = frame_len // block_len
    key_blocks = key_rows.shape[0] // block_len
    listed = block_ids.shape[1]
    group_size = min(query_blocks, max(1, 512 // block_len))
    group_steps = query_blocks // group_size
    score_scale = head_dim ** -0.5
    query_groups = queries.reshape(group_steps, group_size, block_len, head_count, head_dim)
    grad_groups = grads_out.reshape(group_steps, group_size, block_len, head_count, head_dim)
    key_tiles = key_rows.reshape(key_blocks, block_len, head_count, head_dim)
    value_tiles = value_rows.reshape(key_blocks, block_len, head_count, head_dim)
    id_groups = block_ids.astype(jnp.int32).reshape(group_steps, group_size, listed)
    count_groups = counts.astype(jnp.int32).reshape(group_steps, group_size)
    slot_index = jnp.arange(listed, dtype=jnp.int32)

    def one_group(totals, inputs):
        query_group, grad_group, id_group, count_group = inputs
        gathered_keys = key_tiles[id_group].reshape(group_size, listed * block_len, head_count, head_dim)
        gathered_values = value_tiles[id_group].reshape(group_size, listed * block_len, head_count, head_dim)
        live_mask = slot_index[None, :] < count_group[:, None]
        live_mask = jnp.broadcast_to(live_mask[:, :, None], (group_size, listed, block_len))
        live_mask = live_mask.reshape(group_size, 1, 1, listed * block_len)
        scores = product("gqhd,gkhd->ghqk", query_group, gathered_keys) * score_scale
        scores = jnp.where(live_mask, scores, -1e30)
        row_top = jnp.max(scores, axis=-1, keepdims=True)
        row_total = jnp.sum(jnp.exp(scores - row_top), axis=-1, keepdims=True)
        log_total = row_top + jnp.log(row_total)
        probs = jnp.exp(scores - log_total)
        probs_low = probs.astype(jnp.bfloat16)
        attention_out = product("ghqk,gkhd->gqhd", probs_low, gathered_values).astype(jnp.bfloat16)
        deltas = jnp.sum(grad_group.astype(jnp.float32) * attention_out.astype(jnp.float32), axis=-1)
        grad_probs = product("gqhd,gkhd->ghqk", grad_group, gathered_values)
        grad_scores = (probs * (grad_probs - jnp.transpose(deltas, (0, 2, 1))[..., None])).astype(jnp.bfloat16)
        grad_query = product("ghqk,gkhd->gqhd", grad_scores, gathered_keys) * score_scale
        grad_key = product("ghqk,gqhd->gkhd", grad_scores, query_group) * score_scale
        grad_value = product("ghqk,gqhd->gkhd", probs_low, grad_group)
        update = jnp.stack([grad_key, grad_value]).reshape(2, group_size * listed, block_len, width)
        totals = totals.at[:, id_group.reshape(-1)].add(update)
        return totals, grad_query.reshape(group_size * block_len, width)

    start_totals = jnp.zeros((2, key_blocks, block_len, width), jnp.float32)
    totals, grad_rows = lax.scan(one_group, start_totals, (query_groups, grad_groups, id_groups, count_groups))
    return grad_rows.reshape(frame_len, width), totals.reshape(2, key_blocks * block_len, width)


def reference(queries, key_rows, value_rows, grads_out, block_lists, block_counts):
    grad_frames = []
    key_total = jnp.zeros(key_rows.shape, jnp.float32)
    value_total = jnp.zeros(value_rows.shape, jnp.float32)
    for frame_index in range(FRAMES):
        low_frame = max(frame_index - 2, 0)
        high_frame = min(frame_index + 3, FRAMES)
        first_row = frame_index * FRAME
        grad_query, partial_value = band_grads(
            queries[first_row:first_row + FRAME],
            grads_out[first_row:first_row + FRAME],
            key_rows[low_frame * FRAME:high_frame * FRAME],
            value_rows[low_frame * FRAME:high_frame * FRAME],
            block_lists[frame_index] - low_frame * NQB,
            block_counts[frame_index],
            BLK, HD, exact_product)
        grad_frames.append(grad_query.astype(jnp.bfloat16))
        rounded = lax.optimization_barrier(partial_value.astype(jnp.bfloat16)).astype(jnp.float32)
        key_total = key_total.at[low_frame * FRAME:high_frame * FRAME].add(rounded[0])
        value_total = value_total.at[low_frame * FRAME:high_frame * FRAME].add(rounded[1])
    return (jnp.concatenate(grad_frames, axis=0), key_total.astype(jnp.bfloat16), value_total.astype(jnp.bfloat16))
```

```python
import jax
import jax.numpy as jnp
from jax import lax
from jax.experimental import pallas as pl
from jax.experimental.pallas import tpu as pltpu
from jax.sharding import PartitionSpec as P

HD = 128
BLK = 128
SLAB = 8
SCALE = HD**-0.5
LOG2E = 1.4426950408889634
MESH = pl.DeviceIdType.MESH

WINDOW = 48
SEGMENTS = ((0, 5, 0), (12, 3, 5), (22, 3, 8), (32, 1, 11), (40, 1, 12))
SLOTS = 13
FRAME_STEPS = (0,) * 5 + (1,) * 3 + (-1,) * 3 + (2, -2)
BLOCK_STEPS = (-2, -1, 0, 1, 2, -1, 0, 1, -1, 0, 1, 0, 0)
HALO = (
    (0, 8, 32, -2, 0),
    (0, 8, 40, 2, 0),
    (0, 8, 13, -1, 0),
    (0, 8, 23, 1, 0),
    (0, 2, 10, 0, -1),
    (6, 2, 0, 0, 1),
    (0, 1, 21, -1, -1),
    (7, 1, 12, -1, 1),
    (0, 1, 31, 1, -1),
    (7, 1, 22, 1, 1),
)
HALO_START = tuple(sum(entry[1] for entry in HALO[:at]) for at in range(len(HALO)))
HALO_BLOCKS = sum(entry[1] for entry in HALO)
RING_ORDER = (4, 3, 5, 2, 6, 1, 7)


def product(left, right, contract_left, contract_right):
    return lax.dot_general(
        left,
        right,
        (((contract_left,), (contract_right,)), ((), ())),
        preferred_element_type=jnp.float32,
    )


def fold_rows(tile, how):
    return how(tile.reshape(BLK // 8, 8, tile.shape[-1]), axis=0)


def kernel(
    frames,
    slabs,
    heads,
    bias,
    queries,
    keys,
    values,
    grads,
    grad_queries,
    grad_keys,
    grad_values,
    pairs,
    window,
    keys_t,
    totals,
    raw,
    weights,
    part_out,
    part_in,
    query_out,
    key_out,
    in_send,
    in_recv,
    halo_send,
    halo_recv,
    part_send,
    part_recv,
    out_send,
    out_recv,
):
    frame = lax.axis_index("tm")
    space = lax.axis_index("space")
    slab = space // SLAB
    place = lax.rem(space, SLAB)

    def ring(distance):
        there = lax.rem(place + distance, SLAB)
        return there, (frame, slab * SLAB + there)

    def neighbour(frame_step, slab_step):
        to_frame = lax.rem(frame + frame_step + frames, frames)
        to_slab = lax.rem(slab + slab_step + slabs, slabs)
        return (to_frame, to_slab * SLAB + place)

    def head_columns(owner, step):
        return pl.ds(pl.multiple_of((owner * heads + step) * HD, HD), HD)

    def send(source, target, send_sem, recv_sem, device):
        pltpu.make_async_remote_copy(
            src_ref=source,
            dst_ref=target,
            send_sem=send_sem,
            recv_sem=recv_sem,
            device_id=device,
            device_id_type=MESH,
        ).start()

    def wait_for(ref, sem):
        pltpu.make_async_copy(ref, ref, sem).wait()

    def start_inputs(step):
        landing = (
            pairs.at[step, place, 0:BLK, 0:HD],
            pairs.at[step, place, BLK : 2 * BLK, HD : 2 * HD],
            window.at[step, 2 + place, :, 0:HD],
            window.at[step, 2 + place, :, HD : 2 * HD],
        )
        for distance in RING_ORDER:
            there, device = ring(distance)
            for at, source in ((2, keys), (3, values), (0, queries), (1, grads)):
                columns = head_columns(there, step)
                send(source.at[:, columns], landing[at], in_send.at[step], in_recv.at[step, at], device)
        for at, source in enumerate((queries, grads, keys, values)):
            columns = head_columns(place, step)
            pltpu.make_async_copy(source.at[:, columns], landing[at], in_recv.at[step, at]).start()

    def start_halo(step):
        wait_for(window.at[step, 2:10, :, 0:HD], in_recv.at[step, 2])
        wait_for(window.at[step, 2:10, :, HD : 2 * HD], in_recv.at[step, 3])
        for at, (first, count, position, frame_step, slab_step) in enumerate(HALO):
            send(
                window.at[step, 2 + first : 2 + first + count],
                window.at[step, position : position + count],
                halo_send.at[step],
                halo_recv.at[step, at],
                neighbour(frame_step, slab_step),
            )

    def compute(step):
        wait_for(pairs.at[step, :, 0:BLK, 0:HD], in_recv.at[step, 0])
        wait_for(pairs.at[step, :, BLK : 2 * BLK, HD : 2 * HD], in_recv.at[step, 1])
        for at, (_, count, position, _, _) in enumerate(HALO):
            wait_for(window.at[step, position : position + count], halo_recv.at[step, at])

        def prepare(position, carry):
            columns = pl.ds(pl.multiple_of(position * BLK, BLK), BLK)
            keys_t[:, columns] = window[step, position, :, 0:HD].T
            totals[position] = jnp.zeros((BLK, 2 * HD), jnp.float32)
            return carry

        lax.fori_loop(0, WINDOW, prepare, 0)

        def query_block(i, carry):
            pair = pairs[step, i]
            top = jnp.full((8, BLK), -3e38, jnp.float32)
            for base, count, slot in SEGMENTS:
                tiles = window[step, pl.ds(base + i, count)].reshape(count * BLK, 2 * HD)
                both = product(tiles, pair, 1, 1)
                raw[slot * BLK : (slot + count) * BLK, :] = both
                for at in range(count):
                    highest = fold_rows(both[at * BLK : (at + 1) * BLK, 0:BLK], jnp.max)
                    top = jnp.maximum(top, highest * (SCALE * LOG2E) + bias[i, slot + at])
            top = jnp.max(top, axis=0, keepdims=True)
            total = jnp.zeros((8, BLK), jnp.float32)
            delta = jnp.zeros((8, BLK), jnp.float32)
            for slot in range(SLOTS):
                rows = slice(slot * BLK, (slot + 1) * BLK)
                power = jnp.exp2(raw[rows, 0:BLK] * (SCALE * LOG2E) + (bias[i, slot] - top))
                total = total + fold_rows(power, jnp.sum)
                delta = delta + fold_rows(power * raw[rows, BLK : 2 * BLK], jnp.sum)
                raw[rows, 0:BLK] = power
            inverse = 1.0 / jnp.sum(total, axis=0, keepdims=True)
            delta = jnp.sum(delta, axis=0, keepdims=True) * inverse
            for slot in range(SLOTS):
                rows = slice(slot * BLK, (slot + 1) * BLK)
                probs = raw[rows, 0:BLK] * inverse
                grad_scores = probs * (raw[rows, BLK : 2 * BLK] - delta)
                weights[rows, 0:BLK] = grad_scores.astype(jnp.bfloat16)
                weights[rows, BLK : 2 * BLK] = probs.astype(jnp.bfloat16)
            grad_query = jnp.zeros((HD, BLK), jnp.float32)
            for base, count, slot in SEGMENTS:
                rows = slice(slot * BLK, (slot + count) * BLK)
                columns = pl.ds(pl.multiple_of((base + i) * BLK, BLK), count * BLK)
                grad_query = grad_query + product(keys_t[:, columns], weights[rows, 0:BLK], 1, 0)
                update = product(weights[rows, :], pair, 1, 0)
                totals[pl.ds(base + i, count)] += update.reshape(count, BLK, 2 * HD)
            query_out[step, i] = (grad_query * SCALE).T.astype(jnp.bfloat16)
            return carry

        lax.fori_loop(0, SLAB, query_block, 0)

        for at, (_, count, position, frame_step, slab_step) in enumerate(HALO):
            start = HALO_START[at]
            for extra in range(count):
                round_total(totals.at[position + extra], part_out.at[step, start + extra])
            send(
                part_out.at[step, start : start + count],
                part_in.at[step, start : start + count],
                part_send.at[step],
                part_recv.at[step, at],
                neighbour(-frame_step, -slab_step),
            )
        for block in range(SLAB):
            round_total(totals.at[2 + block], key_out.at[step, block])
        start_output(step, 0, grad_queries, lambda block: query_out.at[step, block])

    def round_total(source, target):
        target[:, 0:HD] = (source[:, 0:HD] * SCALE).astype(jnp.bfloat16)
        target[:, HD : 2 * HD] = source[:, HD : 2 * HD].astype(jnp.bfloat16)

    def start_output(step, at, result, tile_of):
        target = result.at[:, head_columns(place, step)]
        for distance in RING_ORDER:
            there, device = ring(distance)
            send(tile_of(there), target, out_send.at[at], out_recv.at[at], device)
        pltpu.make_async_copy(tile_of(place), target, out_recv.at[at]).start()

    def finish(step):
        for at, (_, count, _, _, _) in enumerate(HALO):
            start = HALO_START[at]
            wait_for(part_in.at[step, start : start + count], part_recv.at[step, at])
        for block in range(SLAB):
            summed = key_out[step, block].astype(jnp.float32)
            for at, (first, count, _, _, _) in enumerate(HALO):
                if first <= block < first + count:
                    arrived = part_in[step, HALO_START[at] + block - first]
                    summed = summed + arrived.astype(jnp.float32)
            key_out[step, block] = summed.astype(jnp.bfloat16)
        start_output(step, 1, grad_keys, lambda block: key_out.at[step, block, :, 0:HD])
        start_output(step, 2, grad_values, lambda block: key_out.at[step, block, :, HD : 2 * HD])

    barrier = pltpu.get_barrier_semaphore()
    for distance in range(1, SLAB):
        pl.semaphore_signal(barrier, inc=1, device_id=ring(distance)[1], device_id_type=MESH)
    for _, _, _, frame_step, slab_step in HALO:
        device = neighbour(frame_step, slab_step)
        pl.semaphore_signal(barrier, inc=1, device_id=device, device_id_type=MESH)
    zeros = jnp.zeros((BLK, HD), jnp.bfloat16)

    def clear(at, carry):
        step, block = at // SLAB, lax.rem(at, SLAB)
        pairs[step, block, 0:BLK, HD : 2 * HD] = zeros
        pairs[step, block, BLK : 2 * BLK, 0:HD] = zeros
        return carry

    lax.fori_loop(0, heads * SLAB, clear, 0)
    pl.semaphore_wait(barrier, SLAB - 1 + len(HALO))

    start_inputs(0)
    start_inputs(1)

    def stage(at, carry):
        @pl.when(at < heads)
        def _():
            start_halo(at)

        @pl.when(at + 2 < heads)
        def _():
            start_inputs(at + 2)

        @pl.when((at >= 1) & (at < heads + 1))
        def _():
            compute(at - 1)

        @pl.when(at >= 2)
        def _():
            finish(at - 2)

        return carry

    lax.fori_loop(0, heads + 2, stage, 0)

    for at, result in enumerate((grad_queries, grad_keys, grad_values)):
        wait_for(result, out_recv.at[at])
    sent_tiles = (SLAB - 1) * heads // 2
    for at in range(3):
        wait_for(window.at[0, 0:sent_tiles], out_send.at[at])

    def drain(step, carry):
        wait_for(window.at[step, 0 : (SLAB - 1) * 2], in_send.at[step])
        wait_for(window.at[step, 0:HALO_BLOCKS], halo_send.at[step])
        wait_for(part_in.at[step], part_send.at[step])
        return carry

    lax.fori_loop(0, heads, drain, 0)


def live_bias(block_lists, block_counts, frames):
    frame = lax.axis_index("tm")
    slab = lax.axis_index("space") // SLAB
    frame_blocks = block_lists.shape[1]
    lists = lax.dynamic_slice_in_dim(block_lists[0], slab * SLAB, SLAB, 0)
    counts = lax.dynamic_slice_in_dim(block_counts[0], slab * SLAB, SLAB, 0)
    to_frame = frame + jnp.array(FRAME_STEPS, jnp.int32)[None, :]
    to_block = slab * SLAB + jnp.arange(SLAB)[:, None] + jnp.array(BLOCK_STEPS, jnp.int32)[None, :]
    inside = (to_frame >= 0) & (to_frame < frames) & (to_block >= 0) & (to_block < frame_blocks)
    wanted = to_frame * frame_blocks + to_block
    listed = jnp.arange(lists.shape[1])[None, :] < counts[:, None]
    named = (lists[:, None, :] == wanted[:, :, None]) & listed[:, None, :]
    return jnp.where(inside & jnp.any(named, axis=-1), 0.0, -1e30).astype(jnp.float32)


def solution(mesh):
    frames = mesh.shape["tm"]
    slabs = mesh.shape["space"] // SLAB

    def local(queries, key_rows, value_rows, grads_out, block_lists, block_counts):
        bias = live_bias(block_lists, block_counts, frames)
        rows, width = queries.shape
        heads = width // HD // SLAB
        shape = jax.ShapeDtypeStruct((rows, width), jnp.bfloat16)
        anywhere = pl.BlockSpec(memory_space=pl.ANY)

        def body(*refs):
            kernel(frames, slabs, heads, *refs)

        return pl.pallas_call(
            body,
            out_shape=(shape, shape, shape),
            in_specs=[pl.BlockSpec(memory_space=pltpu.SMEM)] + [anywhere] * 4,
            out_specs=(anywhere, anywhere, anywhere),
            scratch_shapes=[
                pltpu.VMEM((heads, SLAB, 2 * BLK, 2 * HD), jnp.bfloat16),
                pltpu.VMEM((heads, WINDOW, BLK, 2 * HD), jnp.bfloat16),
                pltpu.VMEM((HD, WINDOW * BLK), jnp.bfloat16),
                pltpu.VMEM((WINDOW, BLK, 2 * HD), jnp.float32),
                pltpu.VMEM((SLOTS * BLK, 2 * BLK), jnp.float32),
                pltpu.VMEM((SLOTS * BLK, 2 * BLK), jnp.bfloat16),
                pltpu.VMEM((heads, HALO_BLOCKS, BLK, 2 * HD), jnp.bfloat16),
                pltpu.VMEM((heads, HALO_BLOCKS, BLK, 2 * HD), jnp.bfloat16),
                pltpu.VMEM((heads, SLAB, BLK, HD), jnp.bfloat16),
                pltpu.VMEM((heads, SLAB, BLK, 2 * HD), jnp.bfloat16),
                pltpu.SemaphoreType.DMA((heads,)),
                pltpu.SemaphoreType.DMA((heads, 4)),
                pltpu.SemaphoreType.DMA((heads,)),
                pltpu.SemaphoreType.DMA((heads, len(HALO))),
                pltpu.SemaphoreType.DMA((heads,)),
                pltpu.SemaphoreType.DMA((heads, len(HALO))),
                pltpu.SemaphoreType.DMA((3,)),
                pltpu.SemaphoreType.DMA((3,)),
            ],
            compiler_params=pltpu.CompilerParams(
                collective_id=0, has_side_effects=True, vmem_limit_bytes=60 * 1024 * 1024
            ),
        )(bias, queries, key_rows, value_rows, grads_out)

    rows = P(("tm", "space"), None)
    return jax.shard_map(
        local,
        mesh=mesh,
        in_specs=(rows, rows, rows, rows, P("tm", None, None), P("tm", None)),
        out_specs=(rows, rows, rows),
        check_vma=False,
    )
```

```python
import jax
import jax.numpy as jnp
from jax import lax
from jax.experimental import pallas as pl
from jax.experimental.pallas import tpu as pltpu
from jax.sharding import PartitionSpec as P

HD = 128
BLK = 128
SLAB = 8
SCALE = HD**-0.5
LOG2E = 1.4426950408889634
MESH = pl.DeviceIdType.MESH

WINDOW = 48
SEGMENTS = ((0, 5, 0), (12, 3, 5), (22, 3, 8), (32, 1, 11), (40, 1, 12))
SLOTS = 13
FRAME_STEPS = (0,) * 5 + (1,) * 3 + (-1,) * 3 + (2, -2)
BLOCK_STEPS = (-2, -1, 0, 1, 2, -1, 0, 1, -1, 0, 1, 0, 0)
OUTER, OUTER2, INNER, INNER2 = range(4)


def whole_frame(which, outward):
    return (18 - 5 * outward, 36 - 4 * outward, 18 + 5 * outward, 36 + 4 * outward)[which]


EDGES = (
    (0, 2, 10, 0, -1),
    (6, 2, 0, 0, 1),
    (0, 1, 21, -1, -1),
    (7, 1, 12, -1, 1),
    (0, 1, 31, 1, -1),
    (7, 1, 22, 1, 1),
)
EDGE_START = tuple(24 + sum(entry[1] for entry in EDGES[:at]) for at in range(len(EDGES)))
JOIN = 32
HALO_BLOCKS = 40
PEERS = 4 + len(EDGES)
RING_ORDER = (4, 3, 5, 2, 6, 1, 7)


def product(left, right, contract_left, contract_right):
    return lax.dot_general(
        left,
        right,
        (((contract_left,), (contract_right,)), ((), ())),
        preferred_element_type=jnp.float32,
    )


def fold_rows(tile, how):
    return how(tile.reshape(BLK // 8, 8, tile.shape[-1]), axis=0)


def kernel(
    frames,
    slabs,
    heads,
    block_lists,
    block_counts,
    queries,
    keys,
    values,
    grads,
    grad_queries,
    grad_keys,
    grad_values,
    pairs,
    window,
    keys_t,
    totals,
    raw,
    weights,
    bias,
    part_out,
    part_in,
    query_out,
    key_out,
    in_send,
    in_recv,
    halo_send,
    halo_recv,
    part_send,
    part_recv,
    out_send,
    out_recv,
):
    frame = lax.axis_index("tm")
    space = lax.axis_index("space")
    slab = space // SLAB
    place = lax.rem(space, SLAB)
    outward = 2 * lax.rem(frame, 2) - 1

    def ring(distance):
        there = lax.rem(place + distance, SLAB)
        return there, (frame, slab * SLAB + there)

    def neighbour(frame_step, slab_step):
        to_frame = lax.rem(frame + frame_step + frames, frames)
        to_slab = lax.rem(slab + slab_step + slabs, slabs)
        return (to_frame, to_slab * SLAB + place)

    def head_columns(owner, step):
        return pl.ds(pl.multiple_of((owner * heads + step) * HD, HD), HD)

    def send(source, target, send_sem, recv_sem, device):
        pltpu.make_async_remote_copy(
            src_ref=source,
            dst_ref=target,
            send_sem=send_sem,
            recv_sem=recv_sem,
            device_id=device,
            device_id_type=MESH,
        ).start()

    def wait_for(ref, sem):
        pltpu.make_async_copy(ref, ref, sem).wait()

    def start_inputs(step):
        landing = (
            pairs.at[step, place, 0:BLK, 0:HD],
            pairs.at[step, place, BLK : 2 * BLK, HD : 2 * HD],
            window.at[step, 2 + place, :, 0:HD],
            window.at[step, 2 + place, :, HD : 2 * HD],
        )
        for distance in RING_ORDER:
            there, device = ring(distance)
            for at, source in ((2, keys), (3, values), (0, queries), (1, grads)):
                columns = head_columns(there, step)
                send(source.at[:, columns], landing[at], in_send.at[step], in_recv.at[step, at], device)
        for at, source in enumerate((queries, grads, keys, values)):
            columns = head_columns(place, step)
            pltpu.make_async_copy(source.at[:, columns], landing[at], in_recv.at[step, at]).start()

    def start_halo(step):
        wait_for(window.at[step, 2:10, :, 0:HD], in_recv.at[step, 2])
        wait_for(window.at[step, 2:10, :, HD : 2 * HD], in_recv.at[step, 3])
        own = window.at[step, 2:10]
        for which, distance, there in ((OUTER, 1, -outward), (OUTER2, -2, outward), (INNER, -1, -outward)):
            target = window.at[step, pl.ds(whole_frame(which, there), SLAB)]
            device = neighbour(distance * outward, 0)
            send(own, target, halo_send.at[step], halo_recv.at[step, which], device)
        for at, (first, count, position, frame_step, slab_step) in enumerate(EDGES):
            send(
                window.at[step, 2 + first : 2 + first + count],
                window.at[step, position : position + count],
                halo_send.at[step],
                halo_recv.at[step, 4 + at],
                neighbour(frame_step, slab_step),
            )

    def pass_halo(step):
        arrived = window.at[step, pl.ds(whole_frame(OUTER, outward), SLAB)]
        wait_for(arrived, halo_recv.at[step, OUTER])
        target = window.at[step, pl.ds(whole_frame(INNER2, -outward), SLAB)]
        send(arrived, target, halo_send.at[step], halo_recv.at[step, INNER2], neighbour(-outward, 0))

    def compute(step):
        wait_for(pairs.at[step, :, 0:BLK, 0:HD], in_recv.at[step, 0])
        wait_for(pairs.at[step, :, BLK : 2 * BLK, HD : 2 * HD], in_recv.at[step, 1])
        for which in (OUTER2, INNER, INNER2):
            arrived = window.at[step, pl.ds(whole_frame(which, outward), SLAB)]
            wait_for(arrived, halo_recv.at[step, which])
        for at, (_, count, position, _, _) in enumerate(EDGES):
            wait_for(window.at[step, position : position + count], halo_recv.at[step, 4 + at])

        def prepare(position, carry):
            columns = pl.ds(pl.multiple_of(position * BLK, BLK), BLK)
            keys_t[:, columns] = window[step, position, :, 0:HD].T
            totals[position] = jnp.zeros((BLK, 2 * HD), jnp.float32)
            return carry

        lax.fori_loop(0, WINDOW, prepare, 0)

        def query_block(i, carry):
            @pl.when((i == 1) & (step >= 1))
            def _():
                join_parts(step - 1)

            @pl.when((i == 2) & (step + 1 < heads))
            def _():
                start_halo(step + 1)

            @pl.when((i == 2) & (step + 3 < heads))
            def _():
                start_inputs(step + 3)

            @pl.when((i == 6) & (step + 1 < heads))
            def _():
                pass_halo(step + 1)

            @pl.when((i == 7) & (step >= 1))
            def _():
                finish(step - 1)

            pair = pairs[step, i]
            top = jnp.full((8, BLK), -3e38, jnp.float32)
            for base, count, slot in SEGMENTS:
                tiles = window[step, pl.ds(base + i, count)].reshape(count * BLK, 2 * HD)
                both = product(tiles, pair, 1, 1)
                raw[slot * BLK : (slot + count) * BLK, :] = both
                for at in range(count):
                    highest = fold_rows(both[at * BLK : (at + 1) * BLK, 0:BLK], jnp.max)
                    top = jnp.maximum(top, highest * (SCALE * LOG2E) + bias[i, slot + at])
            top = jnp.max(top, axis=0, keepdims=True)
            total = jnp.zeros((8, BLK), jnp.float32)
            delta = jnp.zeros((8, BLK), jnp.float32)
            for slot in range(SLOTS):
                rows = slice(slot * BLK, (slot + 1) * BLK)
                power = jnp.exp2(raw[rows, 0:BLK] * (SCALE * LOG2E) + (bias[i, slot] - top))
                total = total + fold_rows(power, jnp.sum)
                delta = delta + fold_rows(power * raw[rows, BLK : 2 * BLK], jnp.sum)
                raw[rows, 0:BLK] = power
            inverse = 1.0 / jnp.sum(total, axis=0, keepdims=True)
            delta = jnp.sum(delta, axis=0, keepdims=True) * inverse
            for slot in range(SLOTS):
                rows = slice(slot * BLK, (slot + 1) * BLK)
                probs = raw[rows, 0:BLK] * inverse
                grad_scores = probs * (raw[rows, BLK : 2 * BLK] - delta)
                weights[rows, 0:BLK] = grad_scores.astype(jnp.bfloat16)
                weights[rows, BLK : 2 * BLK] = probs.astype(jnp.bfloat16)
            grad_query = jnp.zeros((HD, BLK), jnp.float32)
            for base, count, slot in SEGMENTS:
                rows = slice(slot * BLK, (slot + count) * BLK)
                columns = pl.ds(pl.multiple_of((base + i) * BLK, BLK), count * BLK)
                grad_query = grad_query + product(keys_t[:, columns], weights[rows, 0:BLK], 1, 0)
                update = product(weights[rows, :], pair, 1, 0)
                totals[pl.ds(base + i, count)] += update.reshape(count, BLK, 2 * HD)
            query_out[step, i] = (grad_query * SCALE).T.astype(jnp.bfloat16)
            return carry

        lax.fori_loop(0, SLAB, query_block, 0)

        def round_frame(which, start):
            def one(block, carry):
                round_total(totals.at[whole_frame(which, outward) + block], part_out.at[step, start + block])
                return carry

            lax.fori_loop(0, SLAB, one, 0)

        round_frame(INNER2, JOIN)
        send_part(step, JOIN, SLAB, INNER2, neighbour(-outward, 0))
        round_frame(OUTER2, 2 * SLAB)
        send_part(step, 2 * SLAB, SLAB, OUTER2, neighbour(2 * outward, 0))
        for at, (_, count, position, frame_step, slab_step) in enumerate(EDGES):
            for extra in range(count):
                round_total(totals.at[position + extra], part_out.at[step, EDGE_START[at] + extra])
            send_part(step, EDGE_START[at], count, 4 + at, neighbour(-frame_step, -slab_step))
        round_frame(INNER, 0)
        send_part(step, 0, SLAB, INNER, neighbour(-outward, 0))
        round_frame(OUTER, SLAB)

        def round_own(block, carry):
            round_total(totals.at[2 + block], key_out.at[step, block])
            return carry

        lax.fori_loop(0, SLAB, round_own, 0)
        start_output(step, 0, grad_queries, lambda block: query_out.at[step, block])

    def send_part(step, start, count, at, device):
        send(
            part_out.at[step, start : start + count],
            part_in.at[step, start : start + count],
            part_send.at[step],
            part_recv.at[step, at],
            device,
        )

    def join_parts(step):
        wait_for(part_in.at[step, JOIN : JOIN + SLAB], part_recv.at[step, INNER2])

        def one(block, carry):
            mine = part_out[step, SLAB + block].astype(jnp.float32)
            other = part_in[step, JOIN + block].astype(jnp.float32)
            part_out[step, SLAB + block] = (mine + other).astype(jnp.bfloat16)
            return carry

        lax.fori_loop(0, SLAB, one, 0)
        send_part(step, SLAB, SLAB, OUTER, neighbour(outward, 0))

    def round_total(source, target):
        target[:, 0:HD] = (source[:, 0:HD] * SCALE).astype(jnp.bfloat16)
        target[:, HD : 2 * HD] = source[:, HD : 2 * HD].astype(jnp.bfloat16)

    def start_output(step, at, result, tile_of):
        target = result.at[:, head_columns(place, step)]
        for distance in RING_ORDER:
            there, device = ring(distance)
            send(tile_of(there), target, out_send.at[at], out_recv.at[at], device)
        pltpu.make_async_copy(tile_of(place), target, out_recv.at[at]).start()

    def finish(step):
        for at, start in ((INNER, 0), (OUTER, SLAB), (OUTER2, 2 * SLAB)):
            wait_for(part_in.at[step, start : start + SLAB], part_recv.at[step, at])
        for at, (_, count, _, _, _) in enumerate(EDGES):
            start = EDGE_START[at]
            wait_for(part_in.at[step, start : start + count], part_recv.at[step, 4 + at])
        for block in range(SLAB):
            summed = key_out[step, block].astype(jnp.float32)
            for start in (0, SLAB, 2 * SLAB):
                summed = summed + part_in[step, start + block].astype(jnp.float32)
            for at, (first, count, _, _, _) in enumerate(EDGES):
                if first <= block < first + count:
                    arrived = part_in[step, EDGE_START[at] + block - first]
                    summed = summed + arrived.astype(jnp.float32)
            key_out[step, block] = summed.astype(jnp.bfloat16)
        start_output(step, 1, grad_keys, lambda block: key_out.at[step, block, :, 0:HD])
        start_output(step, 2, grad_values, lambda block: key_out.at[step, block, :, HD : 2 * HD])

    def find_bias():
        frame_blocks, listed = block_lists.shape[1], block_lists.shape[2]

        def one(i, carry):
            block = slab * SLAB + i
            count = block_counts[0, block]
            named = [jnp.where(at < count, block_lists[0, block, at], -1) for at in range(listed)]
            for slot in range(SLOTS):
                to_frame, to_block = frame + FRAME_STEPS[slot], block + BLOCK_STEPS[slot]
                wanted = to_frame * frame_blocks + to_block
                inside = (to_frame >= 0) & (to_frame < frames) & (to_block >= 0) & (to_block < frame_blocks)
                wanted = jnp.where(inside, wanted, -2)
                live = named[0] == wanted
                for entry in named[1:]:
                    live = live | (entry == wanted)
                bias[i, slot] = jnp.where(live, jnp.float32(0), jnp.float32(-1e30))
            return carry

        lax.fori_loop(0, SLAB, one, 0)

    barrier = pltpu.get_barrier_semaphore()
    for distance in range(1, SLAB):
        pl.semaphore_signal(barrier, inc=1, device_id=ring(distance)[1], device_id_type=MESH)
    steps = [(distance * outward, 0) for distance in (1, 2, -1, -2)]
    for frame_step, slab_step in steps + [entry[3:] for entry in EDGES]:
        device = neighbour(frame_step, slab_step)
        pl.semaphore_signal(barrier, inc=1, device_id=device, device_id_type=MESH)
    zeros = jnp.zeros((BLK, HD), jnp.bfloat16)

    def clear(at, carry):
        step, block = at // SLAB, lax.rem(at, SLAB)
        pairs[step, block, 0:BLK, HD : 2 * HD] = zeros
        pairs[step, block, BLK : 2 * BLK, 0:HD] = zeros
        return carry

    lax.fori_loop(0, heads * SLAB, clear, 0)
    pl.semaphore_wait(barrier, SLAB - 1 + PEERS)

    start_inputs(0)
    start_inputs(1)
    find_bias()
    start_halo(0)
    start_inputs(2)
    pass_halo(0)

    def stage(step, carry):
        compute(step)
        return carry

    lax.fori_loop(0, heads, stage, 0)
    join_parts(heads - 1)
    finish(heads - 1)

    for at, result in enumerate((grad_queries, grad_keys, grad_values)):
        wait_for(result, out_recv.at[at])
    sent_tiles = (SLAB - 1) * heads // 2
    for at in range(3):
        wait_for(window.at[0, 0:sent_tiles], out_send.at[at])

    def drain(step, carry):
        wait_for(window.at[step, 0 : (SLAB - 1) * 2], in_send.at[step])
        wait_for(window.at[step, 0:HALO_BLOCKS], halo_send.at[step])
        wait_for(part_in.at[step], part_send.at[step])
        return carry

    lax.fori_loop(0, heads, drain, 0)


def solution(mesh):
    frames = mesh.shape["tm"]
    slabs = mesh.shape["space"] // SLAB

    def local(queries, key_rows, value_rows, grads_out, block_lists, block_counts):
        rows, width = queries.shape
        heads = width // HD // SLAB
        shape = jax.ShapeDtypeStruct((rows, width), jnp.bfloat16)
        anywhere = pl.BlockSpec(memory_space=pl.ANY)

        def body(*refs):
            kernel(frames, slabs, heads, *refs)

        return pl.pallas_call(
            body,
            out_shape=(shape, shape, shape),
            in_specs=[pl.BlockSpec(memory_space=pltpu.SMEM)] * 2 + [anywhere] * 4,
            out_specs=(anywhere, anywhere, anywhere),
            scratch_shapes=[
                pltpu.VMEM((heads, SLAB, 2 * BLK, 2 * HD), jnp.bfloat16),
                pltpu.VMEM((heads, WINDOW, BLK, 2 * HD), jnp.bfloat16),
                pltpu.VMEM((HD, WINDOW * BLK), jnp.bfloat16),
                pltpu.VMEM((WINDOW, BLK, 2 * HD), jnp.float32),
                pltpu.VMEM((SLOTS * BLK, 2 * BLK), jnp.float32),
                pltpu.VMEM((SLOTS * BLK, 2 * BLK), jnp.bfloat16),
                pltpu.SMEM((SLAB, SLOTS), jnp.float32),
                pltpu.VMEM((heads, HALO_BLOCKS, BLK, 2 * HD), jnp.bfloat16),
                pltpu.VMEM((heads, HALO_BLOCKS, BLK, 2 * HD), jnp.bfloat16),
                pltpu.VMEM((heads, SLAB, BLK, HD), jnp.bfloat16),
                pltpu.VMEM((heads, SLAB, BLK, 2 * HD), jnp.bfloat16),
                pltpu.SemaphoreType.DMA((heads,)),
                pltpu.SemaphoreType.DMA((heads, 4)),
                pltpu.SemaphoreType.DMA((heads,)),
                pltpu.SemaphoreType.DMA((heads, PEERS)),
                pltpu.SemaphoreType.DMA((heads,)),
                pltpu.SemaphoreType.DMA((heads, PEERS)),
                pltpu.SemaphoreType.DMA((3,)),
                pltpu.SemaphoreType.DMA((3,)),
            ],
            compiler_params=pltpu.CompilerParams(
                collective_id=0, has_side_effects=True, vmem_limit_bytes=60 * 1024 * 1024
            ),
        )(block_lists, block_counts, queries, key_rows, value_rows, grads_out)

    rows = P(("tm", "space"), None)
    return jax.shard_map(
        local,
        mesh=mesh,
        in_specs=(rows, rows, rows, rows, P("tm", None, None), P("tm", None)),
        out_specs=(rows, rows, rows),
        check_vma=False,
    )
```

```python
import jax
import jax.numpy as jnp
from jax import lax
from jax.experimental import pallas as pl
from jax.experimental.pallas import tpu as pltpu
from jax.sharding import PartitionSpec as P

HD = 128
BLK = 128
SLAB = 8
SCALE = HD**-0.5
LOG2E = 1.4426950408889634
MESH = pl.DeviceIdType.MESH

WINDOW = 48
SEGMENTS = ((0, 5, 0), (12, 3, 5), (22, 3, 8), (32, 1, 11), (40, 1, 12))
SLOTS = 13
FRAME_STEPS = (0,) * 5 + (1,) * 3 + (-1,) * 3 + (2, -2)
BLOCK_STEPS = (-2, -1, 0, 1, 2, -1, 0, 1, -1, 0, 1, 0, 0)
OUTER, OUTER2, INNER, INNER2 = range(4)


def whole_frame(which, outward):
    return (18 - 5 * outward, 36 - 4 * outward, 18 + 5 * outward, 36 + 4 * outward)[which]


EDGES = (
    (0, 2, 10, 0, -1),
    (6, 2, 0, 0, 1),
    (0, 1, 21, -1, -1),
    (7, 1, 12, -1, 1),
    (0, 1, 31, 1, -1),
    (7, 1, 22, 1, 1),
)
EDGE_AT = 24
HALF = SLAB // 2
OWN_WINDOW = 32
PART_COPIES = 8 + len(EDGES)
JOIN = 32
HALO_BLOCKS = 40
PEERS = 4 + len(EDGES)
RING_ORDER = (4, 3, 5, 2, 6, 1, 7)


def product(left, right, contract_left, contract_right):
    return lax.dot_general(
        left,
        right,
        (((contract_left,), (contract_right,)), ((), ())),
        preferred_element_type=jnp.float32,
    )


def fold_rows(tile, how):
    return how(tile.reshape(BLK // 8, 8, tile.shape[-1]), axis=0)


def kernel(
    frames,
    slabs,
    heads,
    block_lists,
    block_counts,
    queries,
    keys,
    values,
    grads,
    grad_queries,
    grad_keys,
    grad_values,
    pairs,
    window,
    keys_t,
    totals,
    raw,
    weights,
    sums,
    bias,
    part_out,
    part_in,
    query_out,
    key_out,
    in_send,
    in_recv,
    halo_send,
    halo_recv,
    part_send,
    part_recv,
    out_send,
    out_recv,
):
    frame = lax.axis_index("tm")
    space = lax.axis_index("space")
    slab = space // SLAB
    place = lax.rem(space, SLAB)
    outward = 2 * lax.rem(frame, 2) - 1
    backward = lax.rem(slab, 2)

    def ring(distance):
        there = lax.rem(place + distance, SLAB)
        return there, (frame, slab * SLAB + there)

    def neighbour(frame_step, slab_step):
        to_frame = lax.rem(frame + frame_step + frames, frames)
        to_slab = lax.rem(slab + slab_step + slabs, slabs)
        return (to_frame, to_slab * SLAB + place)

    def head_columns(owner, step):
        return pl.ds(pl.multiple_of((owner * heads + step) * HD, HD), HD)

    def send(source, target, send_sem, recv_sem, device):
        pltpu.make_async_remote_copy(
            src_ref=source,
            dst_ref=target,
            send_sem=send_sem,
            recv_sem=recv_sem,
            device_id=device,
            device_id_type=MESH,
        ).start()

    def wait_for(ref, sem):
        pltpu.make_async_copy(ref, ref, sem).wait()

    def start_inputs(step):
        landing = (
            pairs.at[step, place, 0:BLK, 0:HD],
            pairs.at[step, place, BLK : 2 * BLK, HD : 2 * HD],
            window.at[step, 2 + place, :, 0:HD],
            window.at[step, 2 + place, :, HD : 2 * HD],
        )
        for distance in RING_ORDER:
            there, device = ring(distance)
            for at, source in ((2, keys), (3, values), (0, queries), (1, grads)):
                columns = head_columns(there, step)
                send(source.at[:, columns], landing[at], in_send.at[step], in_recv.at[step, at], device)
        for at, source in enumerate((queries, grads, keys, values)):
            columns = head_columns(place, step)
            pltpu.make_async_copy(source.at[:, columns], landing[at], in_recv.at[step, at]).start()

    def start_halo(step):
        wait_for(window.at[step, 2:10, :, 0:HD], in_recv.at[step, 2])
        wait_for(window.at[step, 2:10, :, HD : 2 * HD], in_recv.at[step, 3])
        own = window.at[step, 2:10]
        for which, distance, there in ((OUTER, 1, -outward), (OUTER2, -2, outward), (INNER, -1, -outward)):
            target = window.at[step, pl.ds(whole_frame(which, there), SLAB)]
            device = neighbour(distance * outward, 0)
            send(own, target, halo_send.at[step], halo_recv.at[step, which], device)
        for at, (first, count, position, frame_step, slab_step) in enumerate(EDGES):
            send(
                window.at[step, 2 + first : 2 + first + count],
                window.at[step, position : position + count],
                halo_send.at[step],
                halo_recv.at[step, 4 + at],
                neighbour(frame_step, slab_step),
            )

    def pass_halo(step):
        arrived = window.at[step, pl.ds(whole_frame(OUTER, outward), SLAB)]
        wait_for(arrived, halo_recv.at[step, OUTER])
        target = window.at[step, pl.ds(whole_frame(INNER2, -outward), SLAB)]
        send(arrived, target, halo_send.at[step], halo_recv.at[step, INNER2], neighbour(-outward, 0))

    def compute(step):
        wait_for(pairs.at[step, :, 0:BLK, 0:HD], in_recv.at[step, 0])
        wait_for(pairs.at[step, :, BLK : 2 * BLK, HD : 2 * HD], in_recv.at[step, 1])
        for which in (OUTER2, INNER, INNER2):
            arrived = window.at[step, pl.ds(whole_frame(which, outward), SLAB)]
            wait_for(arrived, halo_recv.at[step, which])
        for at, (_, count, position, _, _) in enumerate(EDGES):
            wait_for(window.at[step, position : position + count], halo_recv.at[step, 4 + at])

        def prepare(position, carry):
            columns = pl.ds(pl.multiple_of(position * BLK, BLK), BLK)
            keys_t[:, columns] = window[step, position, :, 0:HD].T
            return carry

        def clear_total(position, carry):
            totals[position] = jnp.zeros((BLK, 2 * HD), jnp.float32)
            return carry

        lax.fori_loop(0, WINDOW, prepare, 0)
        lax.fori_loop(0, OWN_WINDOW, clear_total, 0)

        def query_block(turn, carry):
            @pl.when((turn == 2) & (step >= 1))
            def _():
                join_parts(step - 1, 1 - backward)

            @pl.when((turn == 2) & (step + 1 < heads))
            def _():
                start_halo(step + 1)

            @pl.when((turn == 2) & (step + 3 < heads))
            def _():
                start_inputs(step + 3)

            @pl.when((turn == 3) & (step >= 1))
            def _():
                finish(step - 1, backward)

            @pl.when((turn == 5) & (step >= 1))
            def _():
                finish(step - 1, 1 - backward)

            @pl.when((turn == 6) & (step + 1 < heads))
            def _():
                pass_halo(step + 1)

            i = turn + backward * (SLAB - 1 - 2 * turn)
            pair = pairs[step, i]
            top = jnp.full((8, BLK), -3e38, jnp.float32)
            for base, count, slot in SEGMENTS:
                tiles = window[step, pl.ds(base + i, count)].reshape(count * BLK, 2 * HD)
                both = product(tiles, pair, 1, 1)
                raw[slot * BLK : (slot + count) * BLK, :] = both
                for at in range(count):
                    highest = fold_rows(both[at * BLK : (at + 1) * BLK, 0:BLK], jnp.max)
                    top = jnp.maximum(top, highest * (SCALE * LOG2E) + bias[i, slot + at])
            top = jnp.max(top, axis=0, keepdims=True)
            total = jnp.zeros((8, BLK), jnp.float32)
            delta = jnp.zeros((8, BLK), jnp.float32)
            for slot in range(SLOTS):
                rows = slice(slot * BLK, (slot + 1) * BLK)
                power = jnp.exp2(raw[rows, 0:BLK] * (SCALE * LOG2E) + (bias[i, slot] - top))
                total = total + fold_rows(power, jnp.sum)
                delta = delta + fold_rows(power * raw[rows, BLK : 2 * BLK], jnp.sum)
                raw[rows, 0:BLK] = power
            inverse = 1.0 / jnp.sum(total, axis=0, keepdims=True)
            delta = jnp.sum(delta, axis=0, keepdims=True) * inverse
            for slot in range(SLOTS):
                rows = slice(slot * BLK, (slot + 1) * BLK)
                probs = raw[rows, 0:BLK] * inverse
                grad_scores = probs * (raw[rows, BLK : 2 * BLK] - delta)
                weights[rows, 0:BLK] = grad_scores.astype(jnp.bfloat16)
                weights[rows, BLK : 2 * BLK] = probs.astype(jnp.bfloat16)
            grad_query = jnp.zeros((HD, BLK), jnp.float32)
            for base, count, slot in SEGMENTS:
                rows = slice(slot * BLK, (slot + count) * BLK)
                columns = pl.ds(pl.multiple_of((base + i) * BLK, BLK), count * BLK)
                grad_query = grad_query + product(keys_t[:, columns], weights[rows, 0:BLK], 1, 0)
                update = product(weights[rows, :], pair, 1, 0)
                if base < OWN_WINDOW:
                    totals[pl.ds(base + i, count)] += update.reshape(count, BLK, 2 * HD)
                else:
                    start = EDGE_AT - SLAB * outward if base == 32 else EDGE_AT + SLAB * outward
                    part_out[step, start + i, :, 0:HD] = (update[:, 0:HD] * SCALE).astype(jnp.bfloat16)
                    part_out[step, start + i, :, HD : 2 * HD] = update[:, HD : 2 * HD].astype(jnp.bfloat16)
            query_out[step, i] = (grad_query * SCALE).T.astype(jnp.bfloat16)
            give(step, 0, grad_queries, query_out.at[step, i], i)

            @pl.when(turn == HALF - 1)
            def _():
                send_far(step, backward)

            @pl.when(turn == HALF + 1)
            def _():
                send_near(step, backward, 1 - backward)
                join_parts(step, backward)

            return carry

        lax.fori_loop(0, SLAB, query_block, 0)

        send_far(step, 1 - backward)
        send_near(step, 1 - backward, backward)

    def send_part(step, start, count, at, device):
        send(
            part_out.at[step, pl.ds(start, count)],
            part_in.at[step, pl.ds(start, count)],
            part_send.at[step],
            part_recv.at[step, at],
            device,
        )

    def send_far(step, half):
        send_part(step, JOIN + HALF * half, HALF, 2 * INNER2 + half, neighbour(-outward, 0))
        send_part(step, 2 * SLAB + HALF * half, HALF, 2 * OUTER2 + half, neighbour(2 * outward, 0))

    def send_near(step, half, side):
        outer, inner = whole_frame(OUTER, outward), whole_frame(INNER, outward)

        def one(at, carry):
            block = HALF * half + at
            round_total(totals.at[outer + block], part_out.at[step, SLAB + block])
            round_total(totals.at[inner + block], part_out.at[step, block])
            round_total(totals.at[2 + block], key_out.at[step, block])
            return carry

        lax.fori_loop(0, HALF, one, 0)
        send_part(step, HALF * half, HALF, 2 * INNER + half, neighbour(-outward, 0))
        for at, count, position, start, frame_step in (
            (8, 2, 10 - 10 * side, EDGE_AT + 2 * side, 0),
            (10, 1, 21 - 9 * side, EDGE_AT + 4 + side, 1),
            (12, 1, 31 - 9 * side, EDGE_AT + 6 + side, -1),
        ):
            for extra in range(count):
                round_total(totals.at[position + extra], part_out.at[step, start + extra])
            send_part(step, start, count, at + side, neighbour(frame_step, 1 - 2 * side))

    def join_parts(step, half):
        wait_for(part_in.at[step, pl.ds(JOIN + HALF * half, HALF)], part_recv.at[step, 2 * INNER2 + half])

        def one(at, carry):
            block = HALF * half + at
            mine = part_out[step, SLAB + block].astype(jnp.float32)
            other = part_in[step, JOIN + block].astype(jnp.float32)
            part_out[step, SLAB + block] = (mine + other).astype(jnp.bfloat16)
            return carry

        lax.fori_loop(0, HALF, one, 0)
        send_part(step, SLAB + HALF * half, HALF, 2 * OUTER + half, neighbour(outward, 0))

    def round_total(source, target):
        target[:, 0:HD] = (source[:, 0:HD] * SCALE).astype(jnp.bfloat16)
        target[:, HD : 2 * HD] = source[:, HD : 2 * HD].astype(jnp.bfloat16)

    def give(step, at, result, tile, there):
        target = result.at[:, head_columns(place, step)]

        @pl.when(there == place)
        def _():
            pltpu.make_async_copy(tile, target, out_recv.at[at]).start()

        @pl.when(there != place)
        def _():
            send(tile, target, out_send.at[at], out_recv.at[at], (frame, slab * SLAB + there))

    def finish(step, half):
        for at, start in ((INNER, 0), (OUTER, SLAB), (OUTER2, 2 * SLAB)):
            arrived = part_in.at[step, pl.ds(start + HALF * half, HALF)]
            wait_for(arrived, part_recv.at[step, 2 * at + half])
        for at, count, start in ((8, 2, EDGE_AT + 2 * half), (10, 1, EDGE_AT + 4 + half), (12, 1, EDGE_AT + 6 + half)):
            wait_for(part_in.at[step, pl.ds(start, count)], part_recv.at[step, at + half])
        for at in range(HALF):
            block = HALF * half + at
            summed = key_out[step, block].astype(jnp.float32)
            for start in (0, SLAB, 2 * SLAB):
                summed = summed + part_in[step, start + block].astype(jnp.float32)
            sums[at] = summed
        for extra in range(2):
            sums[2 * half + extra] += part_in[step, EDGE_AT + 2 * half + extra].astype(jnp.float32)
        for start in (EDGE_AT + 4, EDGE_AT + 6):
            sums[3 * half] += part_in[step, start + half].astype(jnp.float32)
        for at in range(HALF):
            block = HALF * half + at
            key_out[step, block] = sums[at].astype(jnp.bfloat16)
            give(step, 1, grad_keys, key_out.at[step, block, :, 0:HD], block)
            give(step, 2, grad_values, key_out.at[step, block, :, HD : 2 * HD], block)

    def find_bias():
        frame_blocks, listed = block_lists.shape[1], block_lists.shape[2]

        def one(i, carry):
            block = slab * SLAB + i
            count = block_counts[0, block]
            named = [jnp.where(at < count, block_lists[0, block, at], -1) for at in range(listed)]
            for slot in range(SLOTS):
                to_frame, to_block = frame + FRAME_STEPS[slot], block + BLOCK_STEPS[slot]
                wanted = to_frame * frame_blocks + to_block
                inside = (to_frame >= 0) & (to_frame < frames) & (to_block >= 0) & (to_block < frame_blocks)
                wanted = jnp.where(inside, wanted, -2)
                live = named[0] == wanted
                for entry in named[1:]:
                    live = live | (entry == wanted)
                bias[i, slot] = jnp.where(live, jnp.float32(0), jnp.float32(-1e30))
            return carry

        lax.fori_loop(0, SLAB, one, 0)

    barrier = pltpu.get_barrier_semaphore()
    for distance in range(1, SLAB):
        pl.semaphore_signal(barrier, inc=1, device_id=ring(distance)[1], device_id_type=MESH)
    steps = [(distance * outward, 0) for distance in (1, 2, -1, -2)]
    for frame_step, slab_step in steps + [entry[3:] for entry in EDGES]:
        device = neighbour(frame_step, slab_step)
        pl.semaphore_signal(barrier, inc=1, device_id=device, device_id_type=MESH)
    zeros = jnp.zeros((BLK, HD), jnp.bfloat16)

    def clear(at, carry):
        step, block = at // SLAB, lax.rem(at, SLAB)
        pairs[step, block, 0:BLK, HD : 2 * HD] = zeros
        pairs[step, block, BLK : 2 * BLK, 0:HD] = zeros
        return carry

    lax.fori_loop(0, heads * SLAB, clear, 0)
    pl.semaphore_wait(barrier, SLAB - 1 + PEERS)

    start_inputs(0)
    start_inputs(1)
    find_bias()
    start_halo(0)
    start_inputs(2)
    pass_halo(0)

    def stage(step, carry):
        compute(step)
        return carry

    lax.fori_loop(0, heads, stage, 0)
    join_parts(heads - 1, 1 - backward)
    finish(heads - 1, backward)
    finish(heads - 1, 1 - backward)

    for at, result in enumerate((grad_queries, grad_keys, grad_values)):
        wait_for(result, out_recv.at[at])
    sent_tiles = (SLAB - 1) * heads // 2
    for at in range(3):
        wait_for(window.at[0, 0:sent_tiles], out_send.at[at])

    def drain(step, carry):
        wait_for(window.at[step, 0 : (SLAB - 1) * 2], in_send.at[step])
        wait_for(window.at[step, 0:HALO_BLOCKS], halo_send.at[step])
        wait_for(part_in.at[step], part_send.at[step])
        return carry

    lax.fori_loop(0, heads, drain, 0)


def solution(mesh):
    frames = mesh.shape["tm"]
    slabs = mesh.shape["space"] // SLAB

    def local(queries, key_rows, value_rows, grads_out, block_lists, block_counts):
        rows, width = queries.shape
        heads = width // HD // SLAB
        shape = jax.ShapeDtypeStruct((rows, width), jnp.bfloat16)
        anywhere = pl.BlockSpec(memory_space=pl.ANY)

        def body(*refs):
            kernel(frames, slabs, heads, *refs)

        return pl.pallas_call(
            body,
            out_shape=(shape, shape, shape),
            in_specs=[pl.BlockSpec(memory_space=pltpu.SMEM)] * 2 + [anywhere] * 4,
            out_specs=(anywhere, anywhere, anywhere),
            scratch_shapes=[
                pltpu.VMEM((heads, SLAB, 2 * BLK, 2 * HD), jnp.bfloat16),
                pltpu.VMEM((heads, WINDOW, BLK, 2 * HD), jnp.bfloat16),
                pltpu.VMEM((HD, WINDOW * BLK), jnp.bfloat16),
                pltpu.VMEM((OWN_WINDOW, BLK, 2 * HD), jnp.float32),
                pltpu.VMEM((SLOTS * BLK, 2 * BLK), jnp.float32),
                pltpu.VMEM((SLOTS * BLK, 2 * BLK), jnp.bfloat16),
                pltpu.VMEM((HALF, BLK, 2 * HD), jnp.float32),
                pltpu.SMEM((SLAB, SLOTS), jnp.float32),
                pltpu.VMEM((heads, HALO_BLOCKS, BLK, 2 * HD), jnp.bfloat16),
                pltpu.VMEM((heads, HALO_BLOCKS, BLK, 2 * HD), jnp.bfloat16),
                pltpu.VMEM((heads, SLAB, BLK, HD), jnp.bfloat16),
                pltpu.VMEM((heads, SLAB, BLK, 2 * HD), jnp.bfloat16),
                pltpu.SemaphoreType.DMA((heads,)),
                pltpu.SemaphoreType.DMA((heads, 4)),
                pltpu.SemaphoreType.DMA((heads,)),
                pltpu.SemaphoreType.DMA((heads, PEERS)),
                pltpu.SemaphoreType.DMA((heads,)),
                pltpu.SemaphoreType.DMA((heads, PART_COPIES)),
                pltpu.SemaphoreType.DMA((3,)),
                pltpu.SemaphoreType.DMA((3,)),
            ],
            compiler_params=pltpu.CompilerParams(
                collective_id=0, has_side_effects=True, vmem_limit_bytes=60 * 1024 * 1024
            ),
        )(block_lists, block_counts, queries, key_rows, value_rows, grads_out)

    rows = P(("tm", "space"), None)
    return jax.shard_map(
        local,
        mesh=mesh,
        in_specs=(rows, rows, rows, rows, P("tm", None, None), P("tm", None)),
        out_specs=(rows, rows, rows),
        check_vma=False,
    )
```

```python
import jax
import jax.numpy as jnp
from jax import lax
from jax.experimental import pallas as pl
from jax.experimental.pallas import tpu as pltpu
from jax.sharding import PartitionSpec as P

HD = 128
BLK = 128
SLAB = 8
SCALE = HD**-0.5
LOG2E = 1.4426950408889634
MESH = pl.DeviceIdType.MESH

WINDOW = 48
SEGMENTS = ((0, 5, 0), (12, 3, 5), (22, 3, 8), (32, 1, 11), (40, 1, 12))
SLOTS = 13
FRAME_STEPS = (0,) * 5 + (1,) * 3 + (-1,) * 3 + (2, -2)
BLOCK_STEPS = (-2, -1, 0, 1, 2, -1, 0, 1, -1, 0, 1, 0, 0)
OUTER, OUTER2, INNER, INNER2 = range(4)


def whole_frame(which, outward):
    return (18 - 5 * outward, 36 - 4 * outward, 18 + 5 * outward, 36 + 4 * outward)[which]


EDGES = (
    (0, 2, 10, 0, -1),
    (6, 2, 0, 0, 1),
    (0, 1, 21, -1, -1),
    (7, 1, 12, -1, 1),
    (0, 1, 31, 1, -1),
    (7, 1, 22, 1, 1),
)
EDGE_AT = 24
HALF = SLAB // 2
OWN_WINDOW = 32
PART_COPIES = 8 + len(EDGES)
JOIN = 32
HALO_BLOCKS = 40
PEERS = 4 + len(EDGES)
PIECES = 4
RING_ORDER = (4, 3, 5, 2, 6, 1, 7)


def product(left, right, contract_left, contract_right):
    return lax.dot_general(
        left,
        right,
        (((contract_left,), (contract_right,)), ((), ())),
        preferred_element_type=jnp.float32,
    )


def fold_rows(tile, how):
    return how(tile.reshape(BLK // 8, 8, tile.shape[-1]), axis=0)


def kernel(
    frames,
    slabs,
    heads,
    lists_in,
    counts_in,
    queries,
    keys,
    values,
    grads,
    grad_queries,
    grad_keys,
    grad_values,
    pairs,
    window,
    keys_t,
    totals,
    raw,
    weights,
    sums,
    block_lists,
    block_counts,
    bias,
    part_out,
    part_in,
    query_out,
    key_out,
    in_send,
    in_recv,
    halo_send,
    halo_recv,
    part_send,
    part_recv,
    out_send,
    out_recv,
    list_sem,
):
    frame = lax.axis_index("tm")
    space = lax.axis_index("space")
    slab = space // SLAB
    place = lax.rem(space, SLAB)
    outward = 2 * lax.rem(frame, 2) - 1
    backward = lax.rem(slab, 2)

    def ring(distance):
        there = lax.rem(place + distance, SLAB)
        return there, (frame, slab * SLAB + there)

    def neighbour(frame_step, slab_step):
        to_frame = lax.rem(frame + frame_step + frames, frames)
        to_slab = lax.rem(slab + slab_step + slabs, slabs)
        return (to_frame, to_slab * SLAB + place)

    def head_columns(owner, step):
        return pl.ds(pl.multiple_of((owner * heads + step) * HD, HD), HD)

    def send(source, target, send_sem, recv_sem, device):
        pltpu.make_async_remote_copy(
            src_ref=source,
            dst_ref=target,
            send_sem=send_sem,
            recv_sem=recv_sem,
            device_id=device,
            device_id_type=MESH,
        ).start()

    def wait_for(ref, sem):
        pltpu.make_async_copy(ref, ref, sem).wait()

    def start_inputs(step):
        landing = (
            pairs.at[step, place, 0:BLK, 0:HD],
            pairs.at[step, place, BLK : 2 * BLK, HD : 2 * HD],
            window.at[step, 2 + place, :, 0:HD],
            window.at[step, 2 + place, :, HD : 2 * HD],
        )
        for distance in RING_ORDER:
            there, device = ring(distance)
            for at, source in ((2, keys), (3, values), (0, queries), (1, grads)):
                columns = head_columns(there, step)
                send(source.at[:, columns], landing[at], in_send.at[step], in_recv.at[step, at], device)
        for at, source in enumerate((queries, grads, keys, values)):
            columns = head_columns(place, step)
            pltpu.make_async_copy(source.at[:, columns], landing[at], in_recv.at[step, at]).start()

    def start_halo(step):
        wait_for(window.at[step, 2:10, :, 0:HD], in_recv.at[step, 2])
        wait_for(window.at[step, 2:10, :, HD : 2 * HD], in_recv.at[step, 3])
        own = window.at[step, 2:10]
        for which, distance, there in ((OUTER, 1, -outward), (OUTER2, -2, outward), (INNER, -1, -outward)):
            target = window.at[step, pl.ds(whole_frame(which, there), SLAB)]
            device = neighbour(distance * outward, 0)
            send(own, target, halo_send.at[step], halo_recv.at[step, which], device)
        for at, (first, count, position, frame_step, slab_step) in enumerate(EDGES):
            send(
                window.at[step, 2 + first : 2 + first + count],
                window.at[step, position : position + count],
                halo_send.at[step],
                halo_recv.at[step, 4 + at],
                neighbour(frame_step, slab_step),
            )

    def pass_halo(step):
        arrived = window.at[step, pl.ds(whole_frame(OUTER, outward), SLAB)]
        wait_for(arrived, halo_recv.at[step, OUTER])
        target = window.at[step, pl.ds(whole_frame(INNER2, -outward), SLAB)]
        send(arrived, target, halo_send.at[step], halo_recv.at[step, INNER2], neighbour(-outward, 0))

    def compute(step):
        wait_for(pairs.at[step, :, 0:BLK, 0:HD], in_recv.at[step, 0])
        wait_for(pairs.at[step, :, BLK : 2 * BLK, HD : 2 * HD], in_recv.at[step, 1])
        for which in (OUTER2, INNER, INNER2):
            arrived = window.at[step, pl.ds(whole_frame(which, outward), SLAB)]
            wait_for(arrived, halo_recv.at[step, which])
        for at, (_, count, position, _, _) in enumerate(EDGES):
            wait_for(window.at[step, position : position + count], halo_recv.at[step, 4 + at])

        def prepare(position, carry):
            columns = pl.ds(pl.multiple_of(position * BLK, BLK), BLK)
            keys_t[:, columns] = window[step, position, :, 0:HD].T
            return carry

        def clear_total(position, carry):
            totals[position] = jnp.zeros((BLK, 2 * HD), jnp.float32)
            return carry

        lax.fori_loop(0, WINDOW, prepare, 0)
        lax.fori_loop(0, OWN_WINDOW, clear_total, 0)

        def query_block(turn, carry):
            @pl.when((turn == 2) & (step >= 1))
            def _():
                join_parts(step - 1, 1 - backward)

            @pl.when((turn == 2) & (step + 1 < heads))
            def _():
                start_halo(step + 1)

            @pl.when((turn == 2) & (step + 3 < heads))
            def _():
                start_inputs(step + 3)

            @pl.when((turn == 3) & (step >= 1))
            def _():
                finish(step - 1, backward)

            @pl.when((turn == 5) & (step >= 1))
            def _():
                finish(step - 1, 1 - backward)

            @pl.when((turn == 6) & (step + 1 < heads))
            def _():
                pass_halo(step + 1)

            i = turn + backward * (SLAB - 1 - 2 * turn)
            pair = pairs[step, i]
            top = jnp.full((8, BLK), -3e38, jnp.float32)
            for base, count, slot in SEGMENTS:
                tiles = window[step, pl.ds(base + i, count)].reshape(count * BLK, 2 * HD)
                both = product(tiles, pair, 1, 1)
                raw[slot * BLK : (slot + count) * BLK, :] = both
                for at in range(count):
                    highest = fold_rows(both[at * BLK : (at + 1) * BLK, 0:BLK], jnp.max)
                    top = jnp.maximum(top, highest * (SCALE * LOG2E) + bias[i, slot + at])
            top = jnp.max(top, axis=0, keepdims=True)
            total = jnp.zeros((8, BLK), jnp.float32)
            delta = jnp.zeros((8, BLK), jnp.float32)
            for slot in range(SLOTS):
                rows = slice(slot * BLK, (slot + 1) * BLK)
                power = jnp.exp2(raw[rows, 0:BLK] * (SCALE * LOG2E) + (bias[i, slot] - top))
                total = total + fold_rows(power, jnp.sum)
                delta = delta + fold_rows(power * raw[rows, BLK : 2 * BLK], jnp.sum)
                raw[rows, 0:BLK] = power
            inverse = 1.0 / jnp.sum(total, axis=0, keepdims=True)
            delta = jnp.sum(delta, axis=0, keepdims=True) * inverse
            for slot in range(SLOTS):
                rows = slice(slot * BLK, (slot + 1) * BLK)
                probs = raw[rows, 0:BLK] * inverse
                grad_scores = probs * (raw[rows, BLK : 2 * BLK] - delta)
                weights[rows, 0:BLK] = grad_scores.astype(jnp.bfloat16)
                weights[rows, BLK : 2 * BLK] = probs.astype(jnp.bfloat16)
            grad_query = jnp.zeros((HD, BLK), jnp.float32)
            for base, count, slot in SEGMENTS:
                rows = slice(slot * BLK, (slot + count) * BLK)
                columns = pl.ds(pl.multiple_of((base + i) * BLK, BLK), count * BLK)
                grad_query = grad_query + product(keys_t[:, columns], weights[rows, 0:BLK], 1, 0)
                update = product(weights[rows, :], pair, 1, 0)
                if base < OWN_WINDOW:
                    totals[pl.ds(base + i, count)] += update.reshape(count, BLK, 2 * HD)
                else:
                    start = EDGE_AT - SLAB * outward if base == 32 else EDGE_AT + SLAB * outward
                    part_out[step, start + i, :, 0:HD] = (update[:, 0:HD] * SCALE).astype(jnp.bfloat16)
                    part_out[step, start + i, :, HD : 2 * HD] = update[:, HD : 2 * HD].astype(jnp.bfloat16)
            query_out[step, i] = (grad_query * SCALE).T.astype(jnp.bfloat16)
            give(step, 0, grad_queries, query_out.at[step, i], i)

            @pl.when(turn == HALF - 1)
            def _():
                send_far(step, backward)

            @pl.when(turn == HALF + 1)
            def _():
                send_near(step, backward, 1 - backward)
                join_parts(step, backward)

            return carry

        lax.fori_loop(0, SLAB, query_block, 0)

        send_far(step, 1 - backward)
        send_near(step, 1 - backward, backward)

    def send_part(step, start, count, at, device):
        send(
            part_out.at[step, pl.ds(start, count)],
            part_in.at[step, pl.ds(start, count)],
            part_send.at[step],
            part_recv.at[step, at],
            device,
        )

    def send_far(step, half):
        send_part(step, JOIN + HALF * half, HALF, 2 * INNER2 + half, neighbour(-outward, 0))
        send_part(step, 2 * SLAB + HALF * half, HALF, 2 * OUTER2 + half, neighbour(2 * outward, 0))

    def send_near(step, half, side):
        outer, inner = whole_frame(OUTER, outward), whole_frame(INNER, outward)

        def one(at, carry):
            block = HALF * half + at
            round_total(totals.at[outer + block], part_out.at[step, SLAB + block])
            round_total(totals.at[inner + block], part_out.at[step, block])
            round_total(totals.at[2 + block], key_out.at[step, block])
            return carry

        lax.fori_loop(0, HALF, one, 0)
        send_part(step, HALF * half, HALF, 2 * INNER + half, neighbour(-outward, 0))
        for at, count, position, start, frame_step in (
            (8, 2, 10 - 10 * side, EDGE_AT + 2 * side, 0),
            (10, 1, 21 - 9 * side, EDGE_AT + 4 + side, 1),
            (12, 1, 31 - 9 * side, EDGE_AT + 6 + side, -1),
        ):
            for extra in range(count):
                round_total(totals.at[position + extra], part_out.at[step, start + extra])
            send_part(step, start, count, at + side, neighbour(frame_step, 1 - 2 * side))

    def join_parts(step, half):
        wait_for(part_in.at[step, pl.ds(JOIN + HALF * half, HALF)], part_recv.at[step, 2 * INNER2 + half])

        def one(at, carry):
            block = HALF * half + at
            mine = part_out[step, SLAB + block].astype(jnp.float32)
            other = part_in[step, JOIN + block].astype(jnp.float32)
            part_out[step, SLAB + block] = (mine + other).astype(jnp.bfloat16)
            return carry

        lax.fori_loop(0, HALF, one, 0)
        send_part(step, SLAB + HALF * half, HALF, 2 * OUTER + half, neighbour(outward, 0))

    def round_total(source, target):
        target[:, 0:HD] = (source[:, 0:HD] * SCALE).astype(jnp.bfloat16)
        target[:, HD : 2 * HD] = source[:, HD : 2 * HD].astype(jnp.bfloat16)

    def give(step, at, result, tile, there):
        target = result.at[:, head_columns(place, step)]

        @pl.when(there == place)
        def _():
            pltpu.make_async_copy(tile, target, out_recv.at[at]).start()

        @pl.when(there != place)
        def _():
            send(tile, target, out_send.at[at], out_recv.at[at], (frame, slab * SLAB + there))

    def finish(step, half):
        for at, start in ((INNER, 0), (OUTER, SLAB), (OUTER2, 2 * SLAB)):
            arrived = part_in.at[step, pl.ds(start + HALF * half, HALF)]
            wait_for(arrived, part_recv.at[step, 2 * at + half])
        for at, count, start in ((8, 2, EDGE_AT + 2 * half), (10, 1, EDGE_AT + 4 + half), (12, 1, EDGE_AT + 6 + half)):
            wait_for(part_in.at[step, pl.ds(start, count)], part_recv.at[step, at + half])
        for at in range(HALF):
            block = HALF * half + at
            summed = key_out[step, block].astype(jnp.float32)
            for start in (0, SLAB, 2 * SLAB):
                summed = summed + part_in[step, start + block].astype(jnp.float32)
            sums[at] = summed
        for extra in range(2):
            sums[2 * half + extra] += part_in[step, EDGE_AT + 2 * half + extra].astype(jnp.float32)
        for start in (EDGE_AT + 4, EDGE_AT + 6):
            sums[3 * half] += part_in[step, start + half].astype(jnp.float32)
        for at in range(HALF):
            block = HALF * half + at
            key_out[step, block] = sums[at].astype(jnp.bfloat16)
            give(step, 1, grad_keys, key_out.at[step, block, :, 0:HD], block)
            give(step, 2, grad_values, key_out.at[step, block, :, HD : 2 * HD], block)

    def find_bias():
        listed, frame_blocks = block_lists.shape[0], block_lists.shape[2]

        def one(i, carry):
            block = slab * SLAB + i
            count = block_counts[0, block]
            named = [jnp.where(at < count, block_lists[at, 0, block], -1) for at in range(listed)]
            for slot in range(SLOTS):
                to_frame, to_block = frame + FRAME_STEPS[slot], block + BLOCK_STEPS[slot]
                wanted = to_frame * frame_blocks + to_block
                inside = (to_frame >= 0) & (to_frame < frames) & (to_block >= 0) & (to_block < frame_blocks)
                wanted = jnp.where(inside, wanted, -2)
                live = named[0] == wanted
                for entry in named[1:]:
                    live = live | (entry == wanted)
                bias[i, slot] = jnp.where(live, jnp.float32(0), jnp.float32(-1e30))
            return carry

        lax.fori_loop(0, SLAB, one, 0)

    barrier = pltpu.get_barrier_semaphore()
    for distance in range(1, SLAB):
        pl.semaphore_signal(barrier, inc=1, device_id=ring(distance)[1], device_id_type=MESH)
    steps = [(distance * outward, 0) for distance in (1, 2, -1, -2)]
    for frame_step, slab_step in steps + [entry[3:] for entry in EDGES]:
        device = neighbour(frame_step, slab_step)
        pl.semaphore_signal(barrier, inc=1, device_id=device, device_id_type=MESH)
    fetch_lists = pltpu.make_async_copy(lists_in, block_lists, list_sem.at[0])
    fetch_counts = pltpu.make_async_copy(counts_in, block_counts, list_sem.at[1])
    fetch_lists.start()
    fetch_counts.start()
    zeros = jnp.zeros((BLK, HD), jnp.bfloat16)

    def clear(at, carry):
        step, block = at // SLAB, lax.rem(at, SLAB)
        pairs[step, block, 0:BLK, HD : 2 * HD] = zeros
        pairs[step, block, BLK : 2 * BLK, 0:HD] = zeros
        return carry

    pl.semaphore_wait(barrier, SLAB - 1 + PEERS)

    start_inputs(0)
    start_inputs(1)
    lax.fori_loop(0, heads * SLAB, clear, 0)
    fetch_lists.wait()
    fetch_counts.wait()
    find_bias()
    start_halo(0)
    start_inputs(2)
    pass_halo(0)

    def stage(step, carry):
        compute(step)
        return carry

    lax.fori_loop(0, heads, stage, 0)
    join_parts(heads - 1, 1 - backward)
    finish(heads - 1, backward)
    finish(heads - 1, 1 - backward)

    for at, result in enumerate((grad_queries, grad_keys, grad_values)):
        wait_for(result, out_recv.at[at])
    sent_tiles = (SLAB - 1) * heads // 2
    for at in range(3):
        wait_for(window.at[0, 0:sent_tiles], out_send.at[at])

    def drain(step, carry):
        wait_for(window.at[step, 0 : (SLAB - 1) * 2], in_send.at[step])
        wait_for(window.at[step, 0:HALO_BLOCKS], halo_send.at[step])
        wait_for(part_in.at[step], part_send.at[step])
        return carry

    lax.fori_loop(0, heads, drain, 0)


def hand_over(*refs):
    sources, targets, (held, in_sem, out_sem) = refs[:3], refs[3:6], refs[6:]
    rows = held.shape[1] // PIECES
    pieces = [(at, piece, slice(piece * rows, (piece + 1) * rows)) for at in range(3) for piece in range(PIECES)]
    arriving = [
        pltpu.make_async_copy(sources[at].at[span], held.at[at, span], in_sem.at[at, piece]) for at, piece, span in pieces
    ]
    leaving = [
        pltpu.make_async_copy(held.at[at, span], targets[at].at[span], out_sem.at[at, piece]) for at, piece, span in pieces
    ]
    for copy in arriving:
        copy.start()
    for copy, then in zip(arriving, leaving):
        copy.wait()
        then.start()
    for copy in leaving:
        copy.wait()


def solution(mesh):
    frames = mesh.shape["tm"]
    slabs = mesh.shape["space"] // SLAB

    def local(queries, key_rows, value_rows, grads_out, block_lists, block_counts):
        rows, width = queries.shape
        block_lists = jnp.transpose(block_lists, (2, 0, 1))
        heads = width // HD // SLAB
        shape = jax.ShapeDtypeStruct((rows, width), jnp.bfloat16)
        anywhere = pl.BlockSpec(memory_space=pl.ANY)

        def body(*refs):
            kernel(frames, slabs, heads, *refs)

        grads = pl.pallas_call(
            body,
            out_shape=(shape, shape, shape),
            in_specs=[anywhere] * 6,
            out_specs=(anywhere, anywhere, anywhere),
            scratch_shapes=[
                pltpu.VMEM((heads, SLAB, 2 * BLK, 2 * HD), jnp.bfloat16),
                pltpu.VMEM((heads, WINDOW, BLK, 2 * HD), jnp.bfloat16),
                pltpu.VMEM((HD, WINDOW * BLK), jnp.bfloat16),
                pltpu.VMEM((OWN_WINDOW, BLK, 2 * HD), jnp.float32),
                pltpu.VMEM((SLOTS * BLK, 2 * BLK), jnp.float32),
                pltpu.VMEM((SLOTS * BLK, 2 * BLK), jnp.bfloat16),
                pltpu.VMEM((HALF, BLK, 2 * HD), jnp.float32),
                pltpu.SMEM(block_lists.shape, jnp.int32),
                pltpu.SMEM(block_counts.shape, jnp.int32),
                pltpu.SMEM((SLAB, SLOTS), jnp.float32),
                pltpu.VMEM((heads, HALO_BLOCKS, BLK, 2 * HD), jnp.bfloat16),
                pltpu.VMEM((heads, HALO_BLOCKS, BLK, 2 * HD), jnp.bfloat16),
                pltpu.VMEM((heads, SLAB, BLK, HD), jnp.bfloat16),
                pltpu.VMEM((heads, SLAB, BLK, 2 * HD), jnp.bfloat16),
                pltpu.SemaphoreType.DMA((heads,)),
                pltpu.SemaphoreType.DMA((heads, 4)),
                pltpu.SemaphoreType.DMA((heads,)),
                pltpu.SemaphoreType.DMA((heads, PEERS)),
                pltpu.SemaphoreType.DMA((heads,)),
                pltpu.SemaphoreType.DMA((heads, PART_COPIES)),
                pltpu.SemaphoreType.DMA((3,)),
                pltpu.SemaphoreType.DMA((3,)),
                pltpu.SemaphoreType.DMA((2,)),
            ],
            compiler_params=pltpu.CompilerParams(
                collective_id=0, has_side_effects=True, vmem_limit_bytes=60 * 1024 * 1024
            ),
        )(block_lists, block_counts, queries, key_rows, value_rows, grads_out)
        return pl.pallas_call(
            hand_over,
            out_shape=(shape, shape, shape),
            in_specs=[anywhere] * 3,
            out_specs=(anywhere, anywhere, anywhere),
            scratch_shapes=[
                pltpu.VMEM((3, rows, width), jnp.bfloat16),
                pltpu.SemaphoreType.DMA((3, PIECES)),
                pltpu.SemaphoreType.DMA((3, PIECES)),
            ],
            compiler_params=pltpu.CompilerParams(vmem_limit_bytes=60 * 1024 * 1024),
        )(*grads)

    rows = P(("tm", "space"), None)
    return jax.shard_map(
        local,
        mesh=mesh,
        in_specs=(rows, rows, rows, rows, P("tm", None, None), P("tm", None)),
        out_specs=(rows, rows, rows),
        check_vma=False,
    )
```

```python
import jax
import jax.numpy as jnp
from jax import lax
from jax.experimental import pallas as pl
from jax.experimental.pallas import tpu as pltpu
from jax.sharding import PartitionSpec as P

HD = 128
BLK = 128
SLAB = 8
SCALE = HD**-0.5
LOG2E = 1.4426950408889634
MESH = pl.DeviceIdType.MESH

WINDOW = 48
SEGMENTS = ((0, 5, 0), (12, 3, 5), (22, 3, 8), (32, 1, 11), (40, 1, 12))
SLOTS = 13
FRAME_STEPS = (0,) * 5 + (1,) * 3 + (-1,) * 3 + (2, -2)
BLOCK_STEPS = (-2, -1, 0, 1, 2, -1, 0, 1, -1, 0, 1, 0, 0)
OUTER, OUTER2, INNER, INNER2 = range(4)


def whole_frame(which, outward):
    return (18 - 5 * outward, 36 - 4 * outward, 18 + 5 * outward, 36 + 4 * outward)[which]


EDGES = (
    (0, 2, 10, 0, -1),
    (6, 2, 0, 0, 1),
    (0, 1, 21, -1, -1),
    (7, 1, 12, -1, 1),
    (0, 1, 31, 1, -1),
    (7, 1, 22, 1, 1),
)
EDGE_AT = 24
HALF = SLAB // 2
OWN_WINDOW = 32
PART_COPIES = 8 + len(EDGES)
JOIN = 32
HALO_BLOCKS = 40
PEERS = 4 + len(EDGES)
RING_ORDER = (4, 3, 5, 2, 6, 1, 7)


def product(left, right, contract_left, contract_right):
    return lax.dot_general(
        left,
        right,
        (((contract_left,), (contract_right,)), ((), ())),
        preferred_element_type=jnp.float32,
    )


def fold_rows(tile, how):
    return how(tile.reshape(BLK // 8, 8, tile.shape[-1]), axis=0)


def kernel(
    frames,
    slabs,
    heads,
    lists_in,
    counts_in,
    queries,
    keys,
    values,
    grads,
    grad_queries,
    grad_keys,
    grad_values,
    pairs,
    window,
    keys_t,
    totals,
    raw,
    weights,
    sums,
    block_lists,
    block_counts,
    bias,
    part_out,
    part_in,
    query_out,
    key_out,
    in_send,
    in_recv,
    halo_send,
    halo_recv,
    part_send,
    part_recv,
    out_send,
    out_recv,
    list_sem,
):
    frame = lax.axis_index("tm")
    space = lax.axis_index("space")
    slab = space // SLAB
    place = lax.rem(space, SLAB)
    outward = 2 * lax.rem(frame, 2) - 1
    backward = lax.rem(slab, 2)

    def ring(distance):
        there = lax.rem(place + distance, SLAB)
        return there, (frame, slab * SLAB + there)

    def neighbour(frame_step, slab_step):
        to_frame = lax.rem(frame + frame_step + frames, frames)
        to_slab = lax.rem(slab + slab_step + slabs, slabs)
        return (to_frame, to_slab * SLAB + place)

    def head_columns(owner, step):
        return pl.ds(pl.multiple_of((owner * heads + step) * HD, HD), HD)

    def send(source, target, send_sem, recv_sem, device):
        pltpu.make_async_remote_copy(
            src_ref=source,
            dst_ref=target,
            send_sem=send_sem,
            recv_sem=recv_sem,
            device_id=device,
            device_id_type=MESH,
        ).start()

    def wait_for(ref, sem):
        pltpu.make_async_copy(ref, ref, sem).wait()

    def start_inputs(step):
        landing = (
            pairs.at[step, place, 0:BLK, 0:HD],
            pairs.at[step, place, BLK : 2 * BLK, HD : 2 * HD],
            window.at[step, 2 + place, :, 0:HD],
            window.at[step, 2 + place, :, HD : 2 * HD],
        )
        for distance in RING_ORDER:
            there, device = ring(distance)
            for at, source in ((2, keys), (3, values), (0, queries), (1, grads)):
                columns = head_columns(there, step)
                send(source.at[:, columns], landing[at], in_send.at[step], in_recv.at[step, at], device)
        for at, source in enumerate((queries, grads, keys, values)):
            columns = head_columns(place, step)
            pltpu.make_async_copy(source.at[:, columns], landing[at], in_recv.at[step, at]).start()

    def start_halo(step):
        wait_for(window.at[step, 2:10, :, 0:HD], in_recv.at[step, 2])
        wait_for(window.at[step, 2:10, :, HD : 2 * HD], in_recv.at[step, 3])
        own = window.at[step, 2:10]
        for which, distance, there in ((OUTER, 1, -outward), (OUTER2, -2, outward), (INNER, -1, -outward)):
            target = window.at[step, pl.ds(whole_frame(which, there), SLAB)]
            device = neighbour(distance * outward, 0)
            send(own, target, halo_send.at[step], halo_recv.at[step, which], device)
        for at, (first, count, position, frame_step, slab_step) in enumerate(EDGES):
            send(
                window.at[step, 2 + first : 2 + first + count],
                window.at[step, position : position + count],
                halo_send.at[step],
                halo_recv.at[step, 4 + at],
                neighbour(frame_step, slab_step),
            )

    def pass_halo(step):
        arrived = window.at[step, pl.ds(whole_frame(OUTER, outward), SLAB)]
        wait_for(arrived, halo_recv.at[step, OUTER])
        target = window.at[step, pl.ds(whole_frame(INNER2, -outward), SLAB)]
        send(arrived, target, halo_send.at[step], halo_recv.at[step, INNER2], neighbour(-outward, 0))

    def compute(step):
        wait_for(pairs.at[step, :, 0:BLK, 0:HD], in_recv.at[step, 0])
        wait_for(pairs.at[step, :, BLK : 2 * BLK, HD : 2 * HD], in_recv.at[step, 1])
        for which in (OUTER2, INNER, INNER2):
            arrived = window.at[step, pl.ds(whole_frame(which, outward), SLAB)]
            wait_for(arrived, halo_recv.at[step, which])
        for at, (_, count, position, _, _) in enumerate(EDGES):
            wait_for(window.at[step, position : position + count], halo_recv.at[step, 4 + at])

        def prepare(position, carry):
            columns = pl.ds(pl.multiple_of(position * BLK, BLK), BLK)
            keys_t[:, columns] = window[step, position, :, 0:HD].T
            return carry

        def clear_total(position, carry):
            totals[position] = jnp.zeros((BLK, 2 * HD), jnp.float32)
            return carry

        lax.fori_loop(0, WINDOW, prepare, 0)
        lax.fori_loop(0, OWN_WINDOW, clear_total, 0)

        def query_block(turn, carry):
            @pl.when((turn == 2) & (step >= 1))
            def _():
                join_parts(step - 1, 1 - backward)

            @pl.when((turn == 2) & (step + 1 < heads))
            def _():
                start_halo(step + 1)

            @pl.when((turn == 2) & (step + 3 < heads))
            def _():
                start_inputs(step + 3)

            @pl.when((turn == 3) & (step >= 1))
            def _():
                finish(step - 1, backward)

            @pl.when((turn == 5) & (step >= 1))
            def _():
                finish(step - 1, 1 - backward)

            @pl.when((turn == 6) & (step + 1 < heads))
            def _():
                pass_halo(step + 1)

            i = turn + backward * (SLAB - 1 - 2 * turn)
            pair = pairs[step, i]
            top = jnp.full((8, BLK), -3e38, jnp.float32)
            for base, count, slot in SEGMENTS:
                tiles = window[step, pl.ds(base + i, count)].reshape(count * BLK, 2 * HD)
                both = product(tiles, pair, 1, 1)
                raw[slot * BLK : (slot + count) * BLK, :] = both
                for at in range(count):
                    highest = fold_rows(both[at * BLK : (at + 1) * BLK, 0:BLK], jnp.max)
                    top = jnp.maximum(top, highest * (SCALE * LOG2E) + bias[i, slot + at])
            top = jnp.max(top, axis=0, keepdims=True)
            total = jnp.zeros((8, BLK), jnp.float32)
            delta = jnp.zeros((8, BLK), jnp.float32)
            for slot in range(SLOTS):
                rows = slice(slot * BLK, (slot + 1) * BLK)
                power = jnp.exp2(raw[rows, 0:BLK] * (SCALE * LOG2E) + (bias[i, slot] - top))
                total = total + fold_rows(power, jnp.sum)
                delta = delta + fold_rows(power * raw[rows, BLK : 2 * BLK], jnp.sum)
                raw[rows, 0:BLK] = power
            inverse = 1.0 / jnp.sum(total, axis=0, keepdims=True)
            delta = jnp.sum(delta, axis=0, keepdims=True) * inverse
            for slot in range(SLOTS):
                rows = slice(slot * BLK, (slot + 1) * BLK)
                probs = raw[rows, 0:BLK] * inverse
                grad_scores = probs * (raw[rows, BLK : 2 * BLK] - delta)
                weights[rows, 0:BLK] = grad_scores.astype(jnp.bfloat16)
                weights[rows, BLK : 2 * BLK] = probs.astype(jnp.bfloat16)
            grad_query = jnp.zeros((HD, BLK), jnp.float32)
            for base, count, slot in SEGMENTS:
                rows = slice(slot * BLK, (slot + count) * BLK)
                columns = pl.ds(pl.multiple_of((base + i) * BLK, BLK), count * BLK)
                grad_query = grad_query + product(keys_t[:, columns], weights[rows, 0:BLK], 1, 0)
                update = product(weights[rows, :], pair, 1, 0)
                if base < OWN_WINDOW:
                    totals[pl.ds(base + i, count)] += update.reshape(count, BLK, 2 * HD)
                else:
                    start = EDGE_AT - SLAB * outward if base == 32 else EDGE_AT + SLAB * outward
                    part_out[step, start + i, :, 0:HD] = (update[:, 0:HD] * SCALE).astype(jnp.bfloat16)
                    part_out[step, start + i, :, HD : 2 * HD] = update[:, HD : 2 * HD].astype(jnp.bfloat16)
            query_out[step, i] = (grad_query * SCALE).T.astype(jnp.bfloat16)

            @pl.when(turn == HALF - 1)
            def _():
                send_far(step, backward)
                give_queries(step, backward)

            @pl.when(turn == HALF + 1)
            def _():
                send_near(step, backward, 1 - backward)
                join_parts(step, backward)

            return carry

        lax.fori_loop(0, SLAB, query_block, 0)

        send_far(step, 1 - backward)
        send_near(step, 1 - backward, backward)
        give_queries(step, 1 - backward)

    def send_part(step, start, count, at, device):
        send(
            part_out.at[step, pl.ds(start, count)],
            part_in.at[step, pl.ds(start, count)],
            part_send.at[step],
            part_recv.at[step, at],
            device,
        )

    def send_far(step, half):
        send_part(step, JOIN + HALF * half, HALF, 2 * INNER2 + half, neighbour(-outward, 0))
        send_part(step, 2 * SLAB + HALF * half, HALF, 2 * OUTER2 + half, neighbour(2 * outward, 0))

    def send_near(step, half, side):
        outer, inner = whole_frame(OUTER, outward), whole_frame(INNER, outward)

        def one(at, carry):
            block = HALF * half + at
            round_total(totals.at[outer + block], part_out.at[step, SLAB + block])
            round_total(totals.at[inner + block], part_out.at[step, block])
            round_total(totals.at[2 + block], key_out.at[step, block])
            return carry

        lax.fori_loop(0, HALF, one, 0)
        send_part(step, HALF * half, HALF, 2 * INNER + half, neighbour(-outward, 0))
        for at, count, position, start, frame_step in (
            (8, 2, 10 - 10 * side, EDGE_AT + 2 * side, 0),
            (10, 1, 21 - 9 * side, EDGE_AT + 4 + side, 1),
            (12, 1, 31 - 9 * side, EDGE_AT + 6 + side, -1),
        ):
            for extra in range(count):
                round_total(totals.at[position + extra], part_out.at[step, start + extra])
            send_part(step, start, count, at + side, neighbour(frame_step, 1 - 2 * side))

    def join_parts(step, half):
        wait_for(part_in.at[step, pl.ds(JOIN + HALF * half, HALF)], part_recv.at[step, 2 * INNER2 + half])

        def one(at, carry):
            block = HALF * half + at
            mine = part_out[step, SLAB + block].astype(jnp.float32)
            other = part_in[step, JOIN + block].astype(jnp.float32)
            part_out[step, SLAB + block] = (mine + other).astype(jnp.bfloat16)
            return carry

        lax.fori_loop(0, HALF, one, 0)
        send_part(step, SLAB + HALF * half, HALF, 2 * OUTER + half, neighbour(outward, 0))

    def round_total(source, target):
        target[:, 0:HD] = (source[:, 0:HD] * SCALE).astype(jnp.bfloat16)
        target[:, HD : 2 * HD] = source[:, HD : 2 * HD].astype(jnp.bfloat16)

    def give(step, at, result, tile, there):
        target = result.at[:, head_columns(place, step)]

        @pl.when(there == place)
        def _():
            pltpu.make_async_copy(tile, target, out_recv.at[at]).start()

        @pl.when(there != place)
        def _():
            send(tile, target, out_send.at[at], out_recv.at[at], (frame, slab * SLAB + there))

    def give_queries(step, half):
        for at in range(HALF):
            block = HALF * half + lax.rem(place + at, HALF)
            give(step, 0, grad_queries, query_out.at[step, block], block)

    def finish(step, half):
        for at, start in ((INNER, 0), (OUTER, SLAB), (OUTER2, 2 * SLAB)):
            arrived = part_in.at[step, pl.ds(start + HALF * half, HALF)]
            wait_for(arrived, part_recv.at[step, 2 * at + half])
        for at, count, start in ((8, 2, EDGE_AT + 2 * half), (10, 1, EDGE_AT + 4 + half), (12, 1, EDGE_AT + 6 + half)):
            wait_for(part_in.at[step, pl.ds(start, count)], part_recv.at[step, at + half])
        for at in range(HALF):
            block = HALF * half + at
            summed = key_out[step, block].astype(jnp.float32)
            for start in (0, SLAB, 2 * SLAB):
                summed = summed + part_in[step, start + block].astype(jnp.float32)
            sums[at] = summed
        for extra in range(2):
            sums[2 * half + extra] += part_in[step, EDGE_AT + 2 * half + extra].astype(jnp.float32)
        for start in (EDGE_AT + 4, EDGE_AT + 6):
            sums[3 * half] += part_in[step, start + half].astype(jnp.float32)
        for at in range(HALF):
            key_out[step, HALF * half + at] = sums[at].astype(jnp.bfloat16)
        for at in range(HALF):
            block = HALF * half + lax.rem(place + at, HALF)
            give(step, 1, grad_keys, key_out.at[step, block, :, 0:HD], block)
            give(step, 2, grad_values, key_out.at[step, block, :, HD : 2 * HD], block)

    def find_bias():
        listed, frame_blocks = block_lists.shape[0], block_lists.shape[2]

        def one(i, carry):
            block = slab * SLAB + i
            count = block_counts[0, block]
            named = [jnp.where(at < count, block_lists[at, 0, block], -1) for at in range(listed)]
            for slot in range(SLOTS):
                to_frame, to_block = frame + FRAME_STEPS[slot], block + BLOCK_STEPS[slot]
                wanted = to_frame * frame_blocks + to_block
                inside = (to_frame >= 0) & (to_frame < frames) & (to_block >= 0) & (to_block < frame_blocks)
                wanted = jnp.where(inside, wanted, -2)
                live = named[0] == wanted
                for entry in named[1:]:
                    live = live | (entry == wanted)
                bias[i, slot] = jnp.where(live, jnp.float32(0), jnp.float32(-1e30))
            return carry

        lax.fori_loop(0, SLAB, one, 0)

    barrier = pltpu.get_barrier_semaphore()
    for distance in range(1, SLAB):
        pl.semaphore_signal(barrier, inc=1, device_id=ring(distance)[1], device_id_type=MESH)
    steps = [(distance * outward, 0) for distance in (1, 2, -1, -2)]
    for frame_step, slab_step in steps + [entry[3:] for entry in EDGES]:
        device = neighbour(frame_step, slab_step)
        pl.semaphore_signal(barrier, inc=1, device_id=device, device_id_type=MESH)
    fetch_lists = pltpu.make_async_copy(lists_in, block_lists, list_sem.at[0])
    fetch_counts = pltpu.make_async_copy(counts_in, block_counts, list_sem.at[1])
    fetch_lists.start()
    fetch_counts.start()
    zeros = jnp.zeros((BLK, HD), jnp.bfloat16)

    def clear(at, carry):
        step, block = at // SLAB, lax.rem(at, SLAB)
        pairs[step, block, 0:BLK, HD : 2 * HD] = zeros
        pairs[step, block, BLK : 2 * BLK, 0:HD] = zeros
        return carry

    pl.semaphore_wait(barrier, SLAB - 1 + PEERS)

    start_inputs(0)
    start_inputs(1)
    lax.fori_loop(0, heads * SLAB, clear, 0)
    fetch_lists.wait()
    fetch_counts.wait()
    find_bias()
    start_halo(0)
    start_inputs(2)
    pass_halo(0)

    def stage(step, carry):
        compute(step)
        return carry

    lax.fori_loop(0, heads, stage, 0)
    join_parts(heads - 1, 1 - backward)
    finish(heads - 1, backward)
    finish(heads - 1, 1 - backward)

    for at, result in enumerate((grad_queries, grad_keys, grad_values)):
        wait_for(result, out_recv.at[at])
    sent_tiles = (SLAB - 1) * heads // 2
    for at in range(3):
        wait_for(window.at[0, 0:sent_tiles], out_send.at[at])

    def drain(step, carry):
        wait_for(window.at[step, 0 : (SLAB - 1) * 2], in_send.at[step])
        wait_for(window.at[step, 0:HALO_BLOCKS], halo_send.at[step])
        wait_for(part_in.at[step], part_send.at[step])
        return carry

    lax.fori_loop(0, heads, drain, 0)


def hand_over(*refs):
    sources, targets, sem = refs[:3], refs[3:6], refs[6]
    copies = [pltpu.make_async_copy(sources[at], targets[at], sem.at[at]) for at in range(3)]
    for copy in copies:
        copy.start()
    for copy in copies:
        copy.wait()


def solution(mesh):
    frames = mesh.shape["tm"]
    slabs = mesh.shape["space"] // SLAB

    def local(queries, key_rows, value_rows, grads_out, block_lists, block_counts):
        rows, width = queries.shape
        block_lists = jnp.transpose(block_lists, (2, 0, 1))
        heads = width // HD // SLAB
        shape = jax.ShapeDtypeStruct((rows, width), jnp.bfloat16)
        anywhere = pl.BlockSpec(memory_space=pl.ANY)
        vmem = pl.BlockSpec(memory_space=pltpu.VMEM)

        def body(*refs):
            kernel(frames, slabs, heads, *refs)

        grads = pl.pallas_call(
            body,
            out_shape=(pltpu.VMEM((rows, width), jnp.bfloat16),) * 3,
            in_specs=[anywhere] * 6,
            out_specs=(vmem, vmem, vmem),
            scratch_shapes=[
                pltpu.VMEM((heads, SLAB, 2 * BLK, 2 * HD), jnp.bfloat16),
                pltpu.VMEM((heads, WINDOW, BLK, 2 * HD), jnp.bfloat16),
                pltpu.VMEM((HD, WINDOW * BLK), jnp.bfloat16),
                pltpu.VMEM((OWN_WINDOW, BLK, 2 * HD), jnp.float32),
                pltpu.VMEM((SLOTS * BLK, 2 * BLK), jnp.float32),
                pltpu.VMEM((SLOTS * BLK, 2 * BLK), jnp.bfloat16),
                pltpu.VMEM((HALF, BLK, 2 * HD), jnp.float32),
                pltpu.SMEM(block_lists.shape, jnp.int32),
                pltpu.SMEM(block_counts.shape, jnp.int32),
                pltpu.SMEM((SLAB, SLOTS), jnp.float32),
                pltpu.VMEM((heads, HALO_BLOCKS, BLK, 2 * HD), jnp.bfloat16),
                pltpu.VMEM((heads, HALO_BLOCKS, BLK, 2 * HD), jnp.bfloat16),
                pltpu.VMEM((heads, SLAB, BLK, HD), jnp.bfloat16),
                pltpu.VMEM((heads, SLAB, BLK, 2 * HD), jnp.bfloat16),
                pltpu.SemaphoreType.DMA((heads,)),
                pltpu.SemaphoreType.DMA((heads, 4)),
                pltpu.SemaphoreType.DMA((heads,)),
                pltpu.SemaphoreType.DMA((heads, PEERS)),
                pltpu.SemaphoreType.DMA((heads,)),
                pltpu.SemaphoreType.DMA((heads, PART_COPIES)),
                pltpu.SemaphoreType.DMA((3,)),
                pltpu.SemaphoreType.DMA((3,)),
                pltpu.SemaphoreType.DMA((2,)),
            ],
            compiler_params=pltpu.CompilerParams(
                collective_id=0, has_side_effects=True, vmem_limit_bytes=60 * 1024 * 1024
            ),
        )(block_lists, block_counts, queries, key_rows, value_rows, grads_out)
        return pl.pallas_call(
            hand_over,
            out_shape=(shape, shape, shape),
            in_specs=[vmem] * 3,
            out_specs=(anywhere, anywhere, anywhere),
            scratch_shapes=[pltpu.SemaphoreType.DMA((3,))],
            compiler_params=pltpu.CompilerParams(vmem_limit_bytes=32 * 1024 * 1024),
        )(*[pltpu.with_memory_space_constraint(grad, pltpu.VMEM) for grad in grads])

    rows = P(("tm", "space"), None)
    return jax.shard_map(
        local,
        mesh=mesh,
        in_specs=(rows, rows, rows, rows, P("tm", None, None), P("tm", None)),
        out_specs=(rows, rows, rows),
        check_vma=False,
    )
```

```python
import jax
import jax.numpy as jnp
from jax import lax
from jax.experimental import pallas as pl
from jax.experimental.pallas import tpu as pltpu
from jax.sharding import PartitionSpec as P

HD = 128
BLK = 128
SLAB = 8
SCALE = HD**-0.5
LOG2E = 1.4426950408889634
MESH = pl.DeviceIdType.MESH

WINDOW = 48
SEGMENTS = ((0, 5, 0), (12, 3, 5), (22, 3, 8), (32, 1, 11), (40, 1, 12))
SLOTS = 13
FRAME_STEPS = (0,) * 5 + (1,) * 3 + (-1,) * 3 + (2, -2)
BLOCK_STEPS = (-2, -1, 0, 1, 2, -1, 0, 1, -1, 0, 1, 0, 0)
OUTER, OUTER2, INNER, INNER2 = range(4)


def whole_frame(which, outward):
    return (18 - 5 * outward, 36 - 4 * outward, 18 + 5 * outward, 36 + 4 * outward)[which]


EDGES = (
    (0, 2, 10, 0, -1),
    (6, 2, 0, 0, 1),
    (0, 1, 21, -1, -1),
    (7, 1, 12, -1, 1),
    (0, 1, 31, 1, -1),
    (7, 1, 22, 1, 1),
)
EDGE_AT = 24
HALF = SLAB // 2
OWN_WINDOW = 32
PART_COPIES = 8 + len(EDGES)
JOIN = 32
HALO_BLOCKS = 40
PEERS = 4 + len(EDGES)
RING_ORDER = (4, 3, 5, 2, 6, 1, 7)


def product(left, right, contract_left, contract_right):
    return lax.dot_general(
        left,
        right,
        (((contract_left,), (contract_right,)), ((), ())),
        preferred_element_type=jnp.float32,
    )


def fold_rows(tile, how):
    return how(tile.reshape(BLK // 8, 8, tile.shape[-1]), axis=0)


def kernel(
    frames,
    slabs,
    heads,
    lists_in,
    counts_in,
    queries,
    keys,
    values,
    grads,
    grad_queries,
    grad_keys,
    grad_values,
    pairs,
    window,
    keys_t,
    totals,
    raw,
    weights,
    sums,
    block_lists,
    block_counts,
    bias,
    part_out,
    part_in,
    query_out,
    key_out,
    in_send,
    in_recv,
    halo_send,
    halo_recv,
    part_send,
    part_recv,
    out_send,
    out_recv,
    list_sem,
):
    frame = lax.axis_index("tm")
    space = lax.axis_index("space")
    slab = space // SLAB
    place = lax.rem(space, SLAB)
    outward = 2 * lax.rem(frame, 2) - 1
    backward = lax.rem(slab, 2)

    def ring(distance):
        there = lax.rem(place + distance, SLAB)
        return there, (frame, slab * SLAB + there)

    def neighbour(frame_step, slab_step):
        to_frame = lax.rem(frame + frame_step + frames, frames)
        to_slab = lax.rem(slab + slab_step + slabs, slabs)
        return (to_frame, to_slab * SLAB + place)

    def head_columns(owner, step):
        return pl.ds(pl.multiple_of((owner * heads + step) * HD, HD), HD)

    def send(source, target, send_sem, recv_sem, device):
        pltpu.make_async_remote_copy(
            src_ref=source,
            dst_ref=target,
            send_sem=send_sem,
            recv_sem=recv_sem,
            device_id=device,
            device_id_type=MESH,
        ).start()

    def wait_for(ref, sem):
        pltpu.make_async_copy(ref, ref, sem).wait()

    def start_inputs(step):
        landing = (
            pairs.at[step, place, 0:BLK, 0:HD],
            pairs.at[step, place, BLK : 2 * BLK, HD : 2 * HD],
            window.at[step, 2 + place, :, 0:HD],
            window.at[step, 2 + place, :, HD : 2 * HD],
        )
        for distance in RING_ORDER:
            there, device = ring(distance)
            for at, source in ((2, keys), (3, values), (0, queries), (1, grads)):
                columns = head_columns(there, step)
                send(source.at[:, columns], landing[at], in_send.at[step], in_recv.at[step, at], device)
        for at, source in enumerate((queries, grads, keys, values)):
            columns = head_columns(place, step)
            pltpu.make_async_copy(source.at[:, columns], landing[at], in_recv.at[step, at]).start()

    def start_halo(step):
        wait_for(window.at[step, 2:10, :, 0:HD], in_recv.at[step, 2])
        wait_for(window.at[step, 2:10, :, HD : 2 * HD], in_recv.at[step, 3])
        own = window.at[step, 2:10]
        for which, distance, there in ((OUTER, 1, -outward), (OUTER2, -2, outward), (INNER, -1, -outward)):
            target = window.at[step, pl.ds(whole_frame(which, there), SLAB)]
            device = neighbour(distance * outward, 0)
            send(own, target, halo_send.at[step], halo_recv.at[step, which], device)
        for at, (first, count, position, frame_step, slab_step) in enumerate(EDGES):
            send(
                window.at[step, 2 + first : 2 + first + count],
                window.at[step, position : position + count],
                halo_send.at[step],
                halo_recv.at[step, 4 + at],
                neighbour(frame_step, slab_step),
            )

    def pass_halo(step):
        arrived = window.at[step, pl.ds(whole_frame(OUTER, outward), SLAB)]
        wait_for(arrived, halo_recv.at[step, OUTER])
        target = window.at[step, pl.ds(whole_frame(INNER2, -outward), SLAB)]
        send(arrived, target, halo_send.at[step], halo_recv.at[step, INNER2], neighbour(-outward, 0))

    def compute(step):
        wait_for(pairs.at[step, :, 0:BLK, 0:HD], in_recv.at[step, 0])
        wait_for(pairs.at[step, :, BLK : 2 * BLK, HD : 2 * HD], in_recv.at[step, 1])
        for which in (OUTER2, INNER, INNER2):
            arrived = window.at[step, pl.ds(whole_frame(which, outward), SLAB)]
            wait_for(arrived, halo_recv.at[step, which])
        for at, (_, count, position, _, _) in enumerate(EDGES):
            wait_for(window.at[step, position : position + count], halo_recv.at[step, 4 + at])

        def prepare(position, carry):
            columns = pl.ds(pl.multiple_of(position * BLK, BLK), BLK)
            keys_t[:, columns] = window[step, position, :, 0:HD].T
            return carry

        def clear_total(position, carry):
            totals[position] = jnp.zeros((BLK, 2 * HD), jnp.float32)
            return carry

        lax.fori_loop(0, WINDOW, prepare, 0)
        lax.fori_loop(0, OWN_WINDOW, clear_total, 0)

        def query_block(turn, carry):
            @pl.when((turn == 2) & (step >= 1))
            def _():
                join_parts(step - 1, 1 - backward)

            @pl.when((turn == 2) & (step + 1 < heads))
            def _():
                start_halo(step + 1)

            @pl.when((turn == 3) & (step >= 1))
            def _():
                finish(step - 1, backward)

            @pl.when((turn == 5) & (step >= 1))
            def _():
                finish(step - 1, 1 - backward)

            @pl.when((turn == 6) & (step + 1 < heads))
            def _():
                pass_halo(step + 1)

            i = turn + backward * (SLAB - 1 - 2 * turn)
            pair = pairs[step, i]
            top = jnp.full((8, BLK), -3e38, jnp.float32)
            for base, count, slot in SEGMENTS:
                tiles = window[step, pl.ds(base + i, count)].reshape(count * BLK, 2 * HD)
                both = product(tiles, pair, 1, 1)
                raw[slot * BLK : (slot + count) * BLK, :] = both
                for at in range(count):
                    highest = fold_rows(both[at * BLK : (at + 1) * BLK, 0:BLK], jnp.max)
                    top = jnp.maximum(top, highest * (SCALE * LOG2E) + bias[i, slot + at])
            top = jnp.max(top, axis=0, keepdims=True)
            total = jnp.zeros((8, BLK), jnp.float32)
            delta = jnp.zeros((8, BLK), jnp.float32)
            for slot in range(SLOTS):
                rows = slice(slot * BLK, (slot + 1) * BLK)
                power = jnp.exp2(raw[rows, 0:BLK] * (SCALE * LOG2E) + (bias[i, slot] - top))
                total = total + fold_rows(power, jnp.sum)
                delta = delta + fold_rows(power * raw[rows, BLK : 2 * BLK], jnp.sum)
                raw[rows, 0:BLK] = power
            inverse = 1.0 / jnp.sum(total, axis=0, keepdims=True)
            delta = jnp.sum(delta, axis=0, keepdims=True) * inverse
            for slot in range(SLOTS):
                rows = slice(slot * BLK, (slot + 1) * BLK)
                probs = raw[rows, 0:BLK] * inverse
                grad_scores = probs * (raw[rows, BLK : 2 * BLK] - delta)
                weights[rows, 0:BLK] = grad_scores.astype(jnp.bfloat16)
                weights[rows, BLK : 2 * BLK] = probs.astype(jnp.bfloat16)
            grad_query = jnp.zeros((HD, BLK), jnp.float32)
            for base, count, slot in SEGMENTS:
                rows = slice(slot * BLK, (slot + count) * BLK)
                columns = pl.ds(pl.multiple_of((base + i) * BLK, BLK), count * BLK)
                grad_query = grad_query + product(keys_t[:, columns], weights[rows, 0:BLK], 1, 0)
                update = product(weights[rows, :], pair, 1, 0)
                if base < OWN_WINDOW:
                    totals[pl.ds(base + i, count)] += update.reshape(count, BLK, 2 * HD)
                else:
                    start = EDGE_AT - SLAB * outward if base == 32 else EDGE_AT + SLAB * outward
                    part_out[step, start + i, :, 0:HD] = (update[:, 0:HD] * SCALE).astype(jnp.bfloat16)
                    part_out[step, start + i, :, HD : 2 * HD] = update[:, HD : 2 * HD].astype(jnp.bfloat16)
            query_out[step, i] = (grad_query * SCALE).T.astype(jnp.bfloat16)

            @pl.when(turn == HALF - 1)
            def _():
                send_far(step, backward)

            @pl.when(turn == HALF + 1)
            def _():
                send_near(step, backward, 1 - backward)
                join_parts(step, backward)

            return carry

        lax.fori_loop(0, SLAB, query_block, 0)

        send_far(step, 1 - backward)
        send_near(step, 1 - backward, backward)
        give_queries(step)

    def send_part(step, start, count, at, device):
        send(
            part_out.at[step, pl.ds(start, count)],
            part_in.at[step, pl.ds(start, count)],
            part_send.at[step],
            part_recv.at[step, at],
            device,
        )

    def send_far(step, half):
        send_part(step, JOIN + HALF * half, HALF, 2 * INNER2 + half, neighbour(-outward, 0))
        send_part(step, 2 * SLAB + HALF * half, HALF, 2 * OUTER2 + half, neighbour(2 * outward, 0))

    def send_near(step, half, side):
        outer, inner = whole_frame(OUTER, outward), whole_frame(INNER, outward)

        def one(at, carry):
            block = HALF * half + at
            round_total(totals.at[outer + block], part_out.at[step, SLAB + block])
            round_total(totals.at[inner + block], part_out.at[step, block])
            round_total(totals.at[2 + block], key_out.at[step, block])
            return carry

        lax.fori_loop(0, HALF, one, 0)
        send_part(step, HALF * half, HALF, 2 * INNER + half, neighbour(-outward, 0))
        for at, count, position, start, frame_step in (
            (8, 2, 10 - 10 * side, EDGE_AT + 2 * side, 0),
            (10, 1, 21 - 9 * side, EDGE_AT + 4 + side, 1),
            (12, 1, 31 - 9 * side, EDGE_AT + 6 + side, -1),
        ):
            for extra in range(count):
                round_total(totals.at[position + extra], part_out.at[step, start + extra])
            send_part(step, start, count, at + side, neighbour(frame_step, 1 - 2 * side))

    def join_parts(step, half):
        wait_for(part_in.at[step, pl.ds(JOIN + HALF * half, HALF)], part_recv.at[step, 2 * INNER2 + half])

        def one(at, carry):
            block = HALF * half + at
            mine = part_out[step, SLAB + block].astype(jnp.float32)
            other = part_in[step, JOIN + block].astype(jnp.float32)
            part_out[step, SLAB + block] = (mine + other).astype(jnp.bfloat16)
            return carry

        lax.fori_loop(0, HALF, one, 0)
        send_part(step, SLAB + HALF * half, HALF, 2 * OUTER + half, neighbour(outward, 0))

    def round_total(source, target):
        target[:, 0:HD] = (source[:, 0:HD] * SCALE).astype(jnp.bfloat16)
        target[:, HD : 2 * HD] = source[:, HD : 2 * HD].astype(jnp.bfloat16)

    def give(step, at, result, tile, there):
        target = result.at[:, head_columns(place, step)]

        @pl.when(there == place)
        def _():
            pltpu.make_async_copy(tile, target, out_recv.at[at]).start()

        @pl.when(there != place)
        def _():
            send(tile, target, out_send.at[at], out_recv.at[at], (frame, slab * SLAB + there))

    def give_queries(step):
        for distance in RING_ORDER + (0,):
            there = lax.rem(place + distance, SLAB)
            give(step, 0, grad_queries, query_out.at[step, there], there)

    def finish(step, half):
        for at, start in ((INNER, 0), (OUTER, SLAB), (OUTER2, 2 * SLAB)):
            arrived = part_in.at[step, pl.ds(start + HALF * half, HALF)]
            wait_for(arrived, part_recv.at[step, 2 * at + half])
        for at, count, start in ((8, 2, EDGE_AT + 2 * half), (10, 1, EDGE_AT + 4 + half), (12, 1, EDGE_AT + 6 + half)):
            wait_for(part_in.at[step, pl.ds(start, count)], part_recv.at[step, at + half])
        for at in range(HALF):
            block = HALF * half + at
            summed = key_out[step, block].astype(jnp.float32)
            for start in (0, SLAB, 2 * SLAB):
                summed = summed + part_in[step, start + block].astype(jnp.float32)
            sums[at] = summed
        for extra in range(2):
            sums[2 * half + extra] += part_in[step, EDGE_AT + 2 * half + extra].astype(jnp.float32)
        for start in (EDGE_AT + 4, EDGE_AT + 6):
            sums[3 * half] += part_in[step, start + half].astype(jnp.float32)
        for at in range(HALF):
            key_out[step, HALF * half + at] = sums[at].astype(jnp.bfloat16)
        for at in range(HALF):
            block = HALF * half + lax.rem(place + at, HALF)
            give(step, 1, grad_keys, key_out.at[step, block, :, 0:HD], block)
            give(step, 2, grad_values, key_out.at[step, block, :, HD : 2 * HD], block)

    def find_bias():
        listed, frame_blocks = block_lists.shape[0], block_lists.shape[2]

        def one(i, carry):
            block = slab * SLAB + i
            count = block_counts[0, block]
            named = [jnp.where(at < count, block_lists[at, 0, block], -1) for at in range(listed)]
            for slot in range(SLOTS):
                to_frame, to_block = frame + FRAME_STEPS[slot], block + BLOCK_STEPS[slot]
                wanted = to_frame * frame_blocks + to_block
                inside = (to_frame >= 0) & (to_frame < frames) & (to_block >= 0) & (to_block < frame_blocks)
                wanted = jnp.where(inside, wanted, -2)
                live = named[0] == wanted
                for entry in named[1:]:
                    live = live | (entry == wanted)
                bias[i, slot] = jnp.where(live, jnp.float32(0), jnp.float32(-1e30))
            return carry

        lax.fori_loop(0, SLAB, one, 0)

    barrier = pltpu.get_barrier_semaphore()
    for distance in range(1, SLAB):
        pl.semaphore_signal(barrier, inc=1, device_id=ring(distance)[1], device_id_type=MESH)
    steps = [(distance * outward, 0) for distance in (1, 2, -1, -2)]
    for frame_step, slab_step in steps + [entry[3:] for entry in EDGES]:
        device = neighbour(frame_step, slab_step)
        pl.semaphore_signal(barrier, inc=1, device_id=device, device_id_type=MESH)
    fetch_lists = pltpu.make_async_copy(lists_in, block_lists, list_sem.at[0])
    fetch_counts = pltpu.make_async_copy(counts_in, block_counts, list_sem.at[1])
    fetch_lists.start()
    fetch_counts.start()
    zeros = jnp.zeros((BLK, HD), jnp.bfloat16)

    def clear(at, carry):
        step, block = at // SLAB, lax.rem(at, SLAB)
        pairs[step, block, 0:BLK, HD : 2 * HD] = zeros
        pairs[step, block, BLK : 2 * BLK, 0:HD] = zeros
        return carry

    pl.semaphore_wait(barrier, SLAB - 1 + PEERS)

    start_inputs(0)
    start_inputs(1)
    start_inputs(2)
    start_inputs(3)
    lax.fori_loop(0, heads * SLAB, clear, 0)
    fetch_lists.wait()
    fetch_counts.wait()
    find_bias()
    start_halo(0)
    pass_halo(0)

    def stage(step, carry):
        compute(step)
        return carry

    lax.fori_loop(0, heads, stage, 0)
    join_parts(heads - 1, 1 - backward)
    finish(heads - 1, backward)
    finish(heads - 1, 1 - backward)

    def drain(step, carry):
        wait_for(window.at[step, 0 : (SLAB - 1) * 2], in_send.at[step])
        wait_for(window.at[step, 0:HALO_BLOCKS], halo_send.at[step])
        wait_for(part_in.at[step], part_send.at[step])
        return carry

    lax.fori_loop(0, heads, drain, 0)

    for at, result in enumerate((grad_queries, grad_keys, grad_values)):
        wait_for(result, out_recv.at[at])
    sent_tiles = (SLAB - 1) * heads // 2
    for at in range(3):
        wait_for(window.at[0, 0:sent_tiles], out_send.at[at])


def hand_over(*refs):
    sources, targets, sem = refs[:3], refs[3:6], refs[6]
    copies = [pltpu.make_async_copy(sources[at], targets[at], sem.at[at]) for at in range(3)]
    for copy in copies:
        copy.start()
    for copy in copies:
        copy.wait()


def solution(mesh):
    frames = mesh.shape["tm"]
    slabs = mesh.shape["space"] // SLAB

    def local(queries, key_rows, value_rows, grads_out, block_lists, block_counts):
        rows, width = queries.shape
        block_lists = jnp.transpose(block_lists, (2, 0, 1))
        heads = width // HD // SLAB
        shape = jax.ShapeDtypeStruct((rows, width), jnp.bfloat16)
        anywhere = pl.BlockSpec(memory_space=pl.ANY)
        vmem = pl.BlockSpec(memory_space=pltpu.VMEM)

        def body(*refs):
            kernel(frames, slabs, heads, *refs)

        grads = pl.pallas_call(
            body,
            out_shape=(pltpu.VMEM((rows, width), jnp.bfloat16),) * 3,
            in_specs=[anywhere] * 6,
            out_specs=(vmem, vmem, vmem),
            scratch_shapes=[
                pltpu.VMEM((heads, SLAB, 2 * BLK, 2 * HD), jnp.bfloat16),
                pltpu.VMEM((heads, WINDOW, BLK, 2 * HD), jnp.bfloat16),
                pltpu.VMEM((HD, WINDOW * BLK), jnp.bfloat16),
                pltpu.VMEM((OWN_WINDOW, BLK, 2 * HD), jnp.float32),
                pltpu.VMEM((SLOTS * BLK, 2 * BLK), jnp.float32),
                pltpu.VMEM((SLOTS * BLK, 2 * BLK), jnp.bfloat16),
                pltpu.VMEM((HALF, BLK, 2 * HD), jnp.float32),
                pltpu.SMEM(block_lists.shape, jnp.int32),
                pltpu.SMEM(block_counts.shape, jnp.int32),
                pltpu.SMEM((SLAB, SLOTS), jnp.float32),
                pltpu.VMEM((heads, HALO_BLOCKS, BLK, 2 * HD), jnp.bfloat16),
                pltpu.VMEM((heads, HALO_BLOCKS, BLK, 2 * HD), jnp.bfloat16),
                pltpu.VMEM((heads, SLAB, BLK, HD), jnp.bfloat16),
                pltpu.VMEM((heads, SLAB, BLK, 2 * HD), jnp.bfloat16),
                pltpu.SemaphoreType.DMA((heads,)),
                pltpu.SemaphoreType.DMA((heads, 4)),
                pltpu.SemaphoreType.DMA((heads,)),
                pltpu.SemaphoreType.DMA((heads, PEERS)),
                pltpu.SemaphoreType.DMA((heads,)),
                pltpu.SemaphoreType.DMA((heads, PART_COPIES)),
                pltpu.SemaphoreType.DMA((3,)),
                pltpu.SemaphoreType.DMA((3,)),
                pltpu.SemaphoreType.DMA((2,)),
            ],
            compiler_params=pltpu.CompilerParams(
                collective_id=0, has_side_effects=True, vmem_limit_bytes=60 * 1024 * 1024
            ),
        )(block_lists, block_counts, queries, key_rows, value_rows, grads_out)
        return pl.pallas_call(
            hand_over,
            out_shape=(shape, shape, shape),
            in_specs=[vmem] * 3,
            out_specs=(anywhere, anywhere, anywhere),
            scratch_shapes=[pltpu.SemaphoreType.DMA((3,))],
            compiler_params=pltpu.CompilerParams(vmem_limit_bytes=32 * 1024 * 1024),
        )(*[pltpu.with_memory_space_constraint(grad, pltpu.VMEM) for grad in grads])

    rows = P(("tm", "space"), None)
    return jax.shard_map(
        local,
        mesh=mesh,
        in_specs=(rows, rows, rows, rows, P("tm", None, None), P("tm", None)),
        out_specs=(rows, rows, rows),
        check_vma=False,
    )
```

```python
import jax
import jax.numpy as jnp
from jax import lax
from jax.experimental import pallas as pl
from jax.experimental.pallas import tpu as pltpu
from jax.sharding import PartitionSpec as P

HD = 128
BLK = 128
SLAB = 8
SCALE = HD**-0.5
LOG2E = 1.4426950408889634
MESH = pl.DeviceIdType.MESH

WINDOW = 48
SEGMENTS = ((0, 5, 0), (12, 3, 5), (22, 3, 8), (32, 1, 11), (40, 1, 12))
SLOTS = 13
FRAME_STEPS = (0,) * 5 + (1,) * 3 + (-1,) * 3 + (2, -2)
BLOCK_STEPS = (-2, -1, 0, 1, 2, -1, 0, 1, -1, 0, 1, 0, 0)
OUTER, OUTER2, INNER, INNER2 = range(4)


def whole_frame(which, outward):
    return (18 - 5 * outward, 36 - 4 * outward, 18 + 5 * outward, 36 + 4 * outward)[which]


EDGES = (
    (0, 2, 10, 0, -1),
    (6, 2, 0, 0, 1),
    (0, 1, 21, -1, -1),
    (7, 1, 12, -1, 1),
    (0, 1, 31, 1, -1),
    (7, 1, 22, 1, 1),
)
EDGE_AT = 24
HALF = SLAB // 2
OWN_WINDOW = 32
PART_COPIES = 8 + len(EDGES)
JOIN = 32
HALO_BLOCKS = 40
PEERS = 4 + len(EDGES)
RING_ORDER = (4, 3, 5, 2, 6, 1, 7)


def product(left, right, contract_left, contract_right):
    return lax.dot_general(
        left,
        right,
        (((contract_left,), (contract_right,)), ((), ())),
        preferred_element_type=jnp.float32,
    )


def fold_rows(tile, how):
    return how(tile.reshape(BLK // 8, 8, tile.shape[-1]), axis=0)


def kernel(
    frames,
    slabs,
    heads,
    lists_in,
    counts_in,
    queries,
    keys,
    values,
    grads,
    grad_queries,
    grad_keys,
    grad_values,
    pairs,
    window,
    keys_t,
    totals,
    raw,
    weights,
    sums,
    block_lists,
    block_counts,
    bias,
    part_out,
    part_in,
    query_out,
    key_out,
    in_send,
    in_recv,
    halo_send,
    halo_recv,
    part_send,
    part_recv,
    out_send,
    out_recv,
    list_sem,
):
    frame = lax.axis_index("tm")
    space = lax.axis_index("space")
    slab = space // SLAB
    place = lax.rem(space, SLAB)
    outward = 2 * lax.rem(frame, 2) - 1
    backward = lax.rem(slab, 2)

    def ring(distance):
        there = lax.rem(place + distance, SLAB)
        return there, (frame, slab * SLAB + there)

    def neighbour(frame_step, slab_step):
        to_frame = lax.rem(frame + frame_step + frames, frames)
        to_slab = lax.rem(slab + slab_step + slabs, slabs)
        return (to_frame, to_slab * SLAB + place)

    def head_columns(owner, step):
        return pl.ds(pl.multiple_of((owner * heads + step) * HD, HD), HD)

    def send(source, target, send_sem, recv_sem, device):
        pltpu.make_async_remote_copy(
            src_ref=source,
            dst_ref=target,
            send_sem=send_sem,
            recv_sem=recv_sem,
            device_id=device,
            device_id_type=MESH,
        ).start()

    def wait_for(ref, sem):
        pltpu.make_async_copy(ref, ref, sem).wait()

    def start_inputs(step):
        landing = (
            pairs.at[step, place, 0:BLK, 0:HD],
            pairs.at[step, place, BLK : 2 * BLK, HD : 2 * HD],
            window.at[step, 2 + place, :, 0:HD],
            window.at[step, 2 + place, :, HD : 2 * HD],
        )
        for group in (((2, keys), (3, values)), ((0, queries), (1, grads))):
            for distance in RING_ORDER:
                there, device = ring(distance)
                columns = head_columns(there, step)
                for at, source in group:
                    send(source.at[:, columns], landing[at], in_send.at[step], in_recv.at[step, at], device)
        for at, source in enumerate((queries, grads, keys, values)):
            columns = head_columns(place, step)
            pltpu.make_async_copy(source.at[:, columns], landing[at], in_recv.at[step, at]).start()

    def start_halo(step):
        wait_for(window.at[step, 2:10, :, 0:HD], in_recv.at[step, 2])
        wait_for(window.at[step, 2:10, :, HD : 2 * HD], in_recv.at[step, 3])
        own = window.at[step, 2:10]
        for which, distance, there in ((OUTER, 1, -outward), (OUTER2, -2, outward), (INNER, -1, -outward)):
            target = window.at[step, pl.ds(whole_frame(which, there), SLAB)]
            device = neighbour(distance * outward, 0)
            send(own, target, halo_send.at[step], halo_recv.at[step, which], device)
        for at, (first, count, position, frame_step, slab_step) in enumerate(EDGES):
            send(
                window.at[step, 2 + first : 2 + first + count],
                window.at[step, position : position + count],
                halo_send.at[step],
                halo_recv.at[step, 4 + at],
                neighbour(frame_step, slab_step),
            )

    def pass_halo(step):
        arrived = window.at[step, pl.ds(whole_frame(OUTER, outward), SLAB)]
        wait_for(arrived, halo_recv.at[step, OUTER])
        target = window.at[step, pl.ds(whole_frame(INNER2, -outward), SLAB)]
        send(arrived, target, halo_send.at[step], halo_recv.at[step, INNER2], neighbour(-outward, 0))

    def compute(step):
        wait_for(pairs.at[step, :, 0:BLK, 0:HD], in_recv.at[step, 0])
        wait_for(pairs.at[step, :, BLK : 2 * BLK, HD : 2 * HD], in_recv.at[step, 1])
        for which in (OUTER2, INNER, INNER2):
            arrived = window.at[step, pl.ds(whole_frame(which, outward), SLAB)]
            wait_for(arrived, halo_recv.at[step, which])
        for at, (_, count, position, _, _) in enumerate(EDGES):
            wait_for(window.at[step, position : position + count], halo_recv.at[step, 4 + at])

        def prepare(position, carry):
            columns = pl.ds(pl.multiple_of(position * BLK, BLK), BLK)
            keys_t[:, columns] = window[step, position, :, 0:HD].T
            return carry

        def clear_total(position, carry):
            totals[position] = jnp.zeros((BLK, 2 * HD), jnp.float32)
            return carry

        lax.fori_loop(0, WINDOW, prepare, 0)
        lax.fori_loop(0, OWN_WINDOW, clear_total, 0)

        def query_block(turn, carry):
            @pl.when((turn == 2) & (step >= 1))
            def _():
                join_parts(step - 1, 1 - backward)

            @pl.when((turn == 2) & (step + 1 < heads))
            def _():
                start_halo(step + 1)

            @pl.when((turn == 2) & (step + 3 < heads))
            def _():
                start_inputs(step + 3)

            @pl.when((turn == 3) & (step >= 1))
            def _():
                finish(step - 1, backward)

            @pl.when((turn == 5) & (step >= 1))
            def _():
                finish(step - 1, 1 - backward)

            @pl.when((turn == 6) & (step + 1 < heads))
            def _():
                pass_halo(step + 1)

            i = turn + backward * (SLAB - 1 - 2 * turn)
            pair = pairs[step, i]
            top = jnp.full((8, BLK), -3e38, jnp.float32)
            for base, count, slot in SEGMENTS:
                tiles = window[step, pl.ds(base + i, count)].reshape(count * BLK, 2 * HD)
                both = product(tiles, pair, 1, 1)
                raw[slot * BLK : (slot + count) * BLK, :] = both
                for at in range(count):
                    highest = fold_rows(both[at * BLK : (at + 1) * BLK, 0:BLK], jnp.max)
                    top = jnp.maximum(top, highest * (SCALE * LOG2E) + bias[i, slot + at])
            top = jnp.max(top, axis=0, keepdims=True)
            total = jnp.zeros((8, BLK), jnp.float32)
            delta = jnp.zeros((8, BLK), jnp.float32)
            for slot in range(SLOTS):
                rows = slice(slot * BLK, (slot + 1) * BLK)
                power = jnp.exp2(raw[rows, 0:BLK] * (SCALE * LOG2E) + (bias[i, slot] - top))
                total = total + fold_rows(power, jnp.sum)
                delta = delta + fold_rows(power * raw[rows, BLK : 2 * BLK], jnp.sum)
                raw[rows, 0:BLK] = power
            inverse = 1.0 / jnp.sum(total, axis=0, keepdims=True)
            delta = jnp.sum(delta, axis=0, keepdims=True) * inverse
            for slot in range(SLOTS):
                rows = slice(slot * BLK, (slot + 1) * BLK)
                probs = raw[rows, 0:BLK] * inverse
                grad_scores = probs * (raw[rows, BLK : 2 * BLK] - delta)
                weights[rows, 0:BLK] = grad_scores.astype(jnp.bfloat16)
                weights[rows, BLK : 2 * BLK] = probs.astype(jnp.bfloat16)
            grad_query = jnp.zeros((HD, BLK), jnp.float32)
            for base, count, slot in SEGMENTS:
                rows = slice(slot * BLK, (slot + count) * BLK)
                columns = pl.ds(pl.multiple_of((base + i) * BLK, BLK), count * BLK)
                grad_query = grad_query + product(keys_t[:, columns], weights[rows, 0:BLK], 1, 0)
                update = product(weights[rows, :], pair, 1, 0)
                if base < OWN_WINDOW:
                    totals[pl.ds(base + i, count)] += update.reshape(count, BLK, 2 * HD)
                else:
                    start = EDGE_AT - SLAB * outward if base == 32 else EDGE_AT + SLAB * outward
                    part_out[step, start + i, :, 0:HD] = (update[:, 0:HD] * SCALE).astype(jnp.bfloat16)
                    part_out[step, start + i, :, HD : 2 * HD] = update[:, HD : 2 * HD].astype(jnp.bfloat16)
            query_out[step, i] = (grad_query * SCALE).T.astype(jnp.bfloat16)

            @pl.when(turn == HALF - 1)
            def _():
                send_far(step, backward)
                give_queries(step, backward)

            @pl.when(turn == HALF + 1)
            def _():
                send_near(step, backward, 1 - backward)
                join_parts(step, backward)

            return carry

        lax.fori_loop(0, SLAB, query_block, 0)

        send_far(step, 1 - backward)
        send_near(step, 1 - backward, backward)
        give_queries(step, 1 - backward)

    def send_part(step, start, count, at, device):
        send(
            part_out.at[step, pl.ds(start, count)],
            part_in.at[step, pl.ds(start, count)],
            part_send.at[step],
            part_recv.at[step, at],
            device,
        )

    def send_far(step, half):
        send_part(step, JOIN + HALF * half, HALF, 2 * INNER2 + half, neighbour(-outward, 0))
        send_part(step, 2 * SLAB + HALF * half, HALF, 2 * OUTER2 + half, neighbour(2 * outward, 0))

    def send_near(step, half, side):
        outer, inner = whole_frame(OUTER, outward), whole_frame(INNER, outward)

        def one(at, carry):
            block = HALF * half + at
            round_total(totals.at[outer + block], part_out.at[step, SLAB + block])
            round_total(totals.at[inner + block], part_out.at[step, block])
            round_total(totals.at[2 + block], key_out.at[step, block])
            return carry

        lax.fori_loop(0, HALF, one, 0)
        send_part(step, HALF * half, HALF, 2 * INNER + half, neighbour(-outward, 0))
        for at, count, position, start, frame_step in (
            (8, 2, 10 - 10 * side, EDGE_AT + 2 * side, 0),
            (10, 1, 21 - 9 * side, EDGE_AT + 4 + side, 1),
            (12, 1, 31 - 9 * side, EDGE_AT + 6 + side, -1),
        ):
            for extra in range(count):
                round_total(totals.at[position + extra], part_out.at[step, start + extra])
            send_part(step, start, count, at + side, neighbour(frame_step, 1 - 2 * side))

    def join_parts(step, half):
        wait_for(part_in.at[step, pl.ds(JOIN + HALF * half, HALF)], part_recv.at[step, 2 * INNER2 + half])

        def one(at, carry):
            block = HALF * half + at
            mine = part_out[step, SLAB + block].astype(jnp.float32)
            other = part_in[step, JOIN + block].astype(jnp.float32)
            part_out[step, SLAB + block] = (mine + other).astype(jnp.bfloat16)
            return carry

        lax.fori_loop(0, HALF, one, 0)
        send_part(step, SLAB + HALF * half, HALF, 2 * OUTER + half, neighbour(outward, 0))

    def round_total(source, target):
        target[:, 0:HD] = (source[:, 0:HD] * SCALE).astype(jnp.bfloat16)
        target[:, HD : 2 * HD] = source[:, HD : 2 * HD].astype(jnp.bfloat16)

    def give(step, at, result, tile, there):
        target = result.at[:, head_columns(place, step)]

        @pl.when(there == place)
        def _():
            pltpu.make_async_copy(tile, target, out_recv.at[at]).start()

        @pl.when(there != place)
        def _():
            send(tile, target, out_send.at[at], out_recv.at[at], (frame, slab * SLAB + there))

    def give_queries(step, half):
        for at in range(HALF):
            block = HALF * half + lax.rem(place + at, HALF)
            give(step, 0, grad_queries, query_out.at[step, block], block)

    def finish(step, half):
        for at, start in ((INNER, 0), (OUTER, SLAB), (OUTER2, 2 * SLAB)):
            arrived = part_in.at[step, pl.ds(start + HALF * half, HALF)]
            wait_for(arrived, part_recv.at[step, 2 * at + half])
        for at, count, start in ((8, 2, EDGE_AT + 2 * half), (10, 1, EDGE_AT + 4 + half), (12, 1, EDGE_AT + 6 + half)):
            wait_for(part_in.at[step, pl.ds(start, count)], part_recv.at[step, at + half])
        for at in range(HALF):
            block = HALF * half + at
            summed = key_out[step, block].astype(jnp.float32)
            for start in (0, SLAB, 2 * SLAB):
                summed = summed + part_in[step, start + block].astype(jnp.float32)
            sums[at] = summed
        for extra in range(2):
            sums[2 * half + extra] += part_in[step, EDGE_AT + 2 * half + extra].astype(jnp.float32)
        for start in (EDGE_AT + 4, EDGE_AT + 6):
            sums[3 * half] += part_in[step, start + half].astype(jnp.float32)
        for at in range(HALF):
            key_out[step, HALF * half + at] = sums[at].astype(jnp.bfloat16)
        for at in range(HALF):
            block = HALF * half + lax.rem(place + at, HALF)
            give(step, 1, grad_keys, key_out.at[step, block, :, 0:HD], block)
            give(step, 2, grad_values, key_out.at[step, block, :, HD : 2 * HD], block)

    def find_bias():
        listed, frame_blocks = block_lists.shape[0], block_lists.shape[2]

        def one(i, carry):
            block = slab * SLAB + i
            count = block_counts[0, block]
            named = [jnp.where(at < count, block_lists[at, 0, block], -1) for at in range(listed)]
            for slot in range(SLOTS):
                to_frame, to_block = frame + FRAME_STEPS[slot], block + BLOCK_STEPS[slot]
                wanted = to_frame * frame_blocks + to_block
                inside = (to_frame >= 0) & (to_frame < frames) & (to_block >= 0) & (to_block < frame_blocks)
                wanted = jnp.where(inside, wanted, -2)
                live = named[0] == wanted
                for entry in named[1:]:
                    live = live | (entry == wanted)
                bias[i, slot] = jnp.where(live, jnp.float32(0), jnp.float32(-1e30))
            return carry

        lax.fori_loop(0, SLAB, one, 0)

    barrier = pltpu.get_barrier_semaphore()
    for distance in range(1, SLAB):
        pl.semaphore_signal(barrier, inc=1, device_id=ring(distance)[1], device_id_type=MESH)
    steps = [(distance * outward, 0) for distance in (1, 2, -1, -2)]
    for frame_step, slab_step in steps + [entry[3:] for entry in EDGES]:
        device = neighbour(frame_step, slab_step)
        pl.semaphore_signal(barrier, inc=1, device_id=device, device_id_type=MESH)
    fetch_lists = pltpu.make_async_copy(lists_in, block_lists, list_sem.at[0])
    fetch_counts = pltpu.make_async_copy(counts_in, block_counts, list_sem.at[1])
    fetch_lists.start()
    fetch_counts.start()
    zeros = jnp.zeros((BLK, HD), jnp.bfloat16)

    def clear(at, carry):
        step, block = at // SLAB, lax.rem(at, SLAB)
        pairs[step, block, 0:BLK, HD : 2 * HD] = zeros
        pairs[step, block, BLK : 2 * BLK, 0:HD] = zeros
        return carry

    pl.semaphore_wait(barrier, SLAB - 1 + PEERS)

    start_inputs(0)
    start_inputs(1)
    lax.fori_loop(0, heads * SLAB, clear, 0)
    fetch_lists.wait()
    fetch_counts.wait()
    find_bias()
    start_halo(0)
    start_inputs(2)
    pass_halo(0)

    def stage(step, carry):
        compute(step)
        return carry

    lax.fori_loop(0, heads, stage, 0)
    join_parts(heads - 1, 1 - backward)
    finish(heads - 1, backward)
    finish(heads - 1, 1 - backward)

    for at, result in enumerate((grad_queries, grad_keys, grad_values)):
        wait_for(result, out_recv.at[at])
    sent_tiles = (SLAB - 1) * heads // 2
    for at in range(3):
        wait_for(window.at[0, 0:sent_tiles], out_send.at[at])

    def drain(step, carry):
        wait_for(window.at[step, 0 : (SLAB - 1) * 2], in_send.at[step])
        wait_for(window.at[step, 0:HALO_BLOCKS], halo_send.at[step])
        wait_for(part_in.at[step], part_send.at[step])
        return carry

    lax.fori_loop(0, heads, drain, 0)


def hand_over(*refs):
    sources, targets, sem = refs[:3], refs[3:6], refs[6]
    copies = [pltpu.make_async_copy(sources[at], targets[at], sem.at[at]) for at in range(3)]
    for copy in copies:
        copy.start()
    for copy in copies:
        copy.wait()


def solution(mesh):
    frames = mesh.shape["tm"]
    slabs = mesh.shape["space"] // SLAB

    def local(queries, key_rows, value_rows, grads_out, block_lists, block_counts):
        rows, width = queries.shape
        block_lists = jnp.transpose(block_lists, (2, 0, 1))
        heads = width // HD // SLAB
        shape = jax.ShapeDtypeStruct((rows, width), jnp.bfloat16)
        anywhere = pl.BlockSpec(memory_space=pl.ANY)
        vmem = pl.BlockSpec(memory_space=pltpu.VMEM)

        def body(*refs):
            kernel(frames, slabs, heads, *refs)

        grads = pl.pallas_call(
            body,
            out_shape=(pltpu.VMEM((rows, width), jnp.bfloat16),) * 3,
            in_specs=[anywhere] * 6,
            out_specs=(vmem, vmem, vmem),
            scratch_shapes=[
                pltpu.VMEM((heads, SLAB, 2 * BLK, 2 * HD), jnp.bfloat16),
                pltpu.VMEM((heads, WINDOW, BLK, 2 * HD), jnp.bfloat16),
                pltpu.VMEM((HD, WINDOW * BLK), jnp.bfloat16),
                pltpu.VMEM((OWN_WINDOW, BLK, 2 * HD), jnp.float32),
                pltpu.VMEM((SLOTS * BLK, 2 * BLK), jnp.float32),
                pltpu.VMEM((SLOTS * BLK, 2 * BLK), jnp.bfloat16),
                pltpu.VMEM((HALF, BLK, 2 * HD), jnp.float32),
                pltpu.SMEM(block_lists.shape, jnp.int32),
                pltpu.SMEM(block_counts.shape, jnp.int32),
                pltpu.SMEM((SLAB, SLOTS), jnp.float32),
                pltpu.VMEM((heads, HALO_BLOCKS, BLK, 2 * HD), jnp.bfloat16),
                pltpu.VMEM((heads, HALO_BLOCKS, BLK, 2 * HD), jnp.bfloat16),
                pltpu.VMEM((heads, SLAB, BLK, HD), jnp.bfloat16),
                pltpu.VMEM((heads, SLAB, BLK, 2 * HD), jnp.bfloat16),
                pltpu.SemaphoreType.DMA((heads,)),
                pltpu.SemaphoreType.DMA((heads, 4)),
                pltpu.SemaphoreType.DMA((heads,)),
                pltpu.SemaphoreType.DMA((heads, PEERS)),
                pltpu.SemaphoreType.DMA((heads,)),
                pltpu.SemaphoreType.DMA((heads, PART_COPIES)),
                pltpu.SemaphoreType.DMA((3,)),
                pltpu.SemaphoreType.DMA((3,)),
                pltpu.SemaphoreType.DMA((2,)),
            ],
            compiler_params=pltpu.CompilerParams(
                collective_id=0, has_side_effects=True, vmem_limit_bytes=60 * 1024 * 1024
            ),
        )(block_lists, block_counts, queries, key_rows, value_rows, grads_out)
        return pl.pallas_call(
            hand_over,
            out_shape=(shape, shape, shape),
            in_specs=[vmem] * 3,
            out_specs=(anywhere, anywhere, anywhere),
            scratch_shapes=[pltpu.SemaphoreType.DMA((3,))],
            compiler_params=pltpu.CompilerParams(vmem_limit_bytes=32 * 1024 * 1024),
        )(*[pltpu.with_memory_space_constraint(grad, pltpu.VMEM) for grad in grads])

    rows = P(("tm", "space"), None)
    return jax.shard_map(
        local,
        mesh=mesh,
        in_specs=(rows, rows, rows, rows, P("tm", None, None), P("tm", None)),
        out_specs=(rows, rows, rows),
        check_vma=False,
    )
```
